32 devices in a mesh: xy: 8 (over z, y), gz: 4 (over x, core).
Axes of the slice: x: 2, y: 2, z: 4, core: 2. Of those that a mesh axis runs over, the one named last changes fastest.
Arguments:
- head_old: float32 [32, 64, 512], P('gz', 'xy'), may hold values from -0.12 to -0.02
- soil_type: int32 [32, 64, 512], P('gz', 'xy'), may hold values from 0 to 11
- soil_table: float32 [5, 12], replicated, may hold values from 0.03 to 2.2, as said below
- land_mask: int32 [64, 512], P('xy'), may hold values 0 or 1
- sun_bin: int32 [64, 512], P('xy'), may hold values from 0 to 23
Outputs:
- head_new: float32 [32, 64, 512], P('gz', 'xy')
The draws below stay inside these ranges and needn't reach their ends.
Inputs may be any that keep to these rules, and one draw needn't show every extreme that they name: `soil_table`: row 0 lies in 0.03 to 0.10, row 1 in 0.35 to 0.50, row 2 in 0.5 to 2.0, row 3 in 1.4 to 2.2, row 4 in 0.3 to 1.0.
All inputs are finite; a program needn't handle non-finite values. No bound on the sum of `land_mask` on one device may be relied on, other than what follows from the above.
Results may differ from the reference program's by a relative error of at most 0.00017.
Values sent between devices are 32-bit elements; how exact they have to be, the bound alone decides.
No kernel may reach another device: no remote copies, remote signals or barrier semaphores. Data moves between devices by JAX's collectives and lax.ppermute only.
A program may use at most 128 MiB of HBM per device.

```python
import math
import jax
import jax.numpy as jnp
from jax import lax

NY = 512
NSOIL = 12
LEVELS = 3
NEWTON = 2
NX = 64
NZ = 32
N_XY = 8
N_GZ = 4


def draw_soil_table(key, part):
    lower_ends = jnp.array([0.03, 0.35, 0.5, 1.4, 0.3], jnp.float32)
    upper_ends = jnp.array([0.1, 0.5, 2.0, 2.2, 1.0], jnp.float32)
    log_rows = jnp.array([0.0, 0.0, 1.0, 0.0, 1.0], jnp.float32)
    fraction = jax.random.uniform(key, (5, NSOIL), jnp.float32)
    linear = lower_ends[:, None] + (upper_ends - lower_ends)[:, None] * fraction
    logged = lower_ends[:, None] * jnp.exp(jnp.log(upper_ends / lower_ends)[:, None] * fraction)
    picked = jnp.where(log_rows[:, None] > 0.5, logged, linear)
    return jnp.clip(picked, lower_ends[:, None], upper_ends[:, None])


def plant(entries, own_key, least, high):
    dims = entries.shape
    spot = [jax.random.randint(jax.random.fold_in(own_key, axis), (), 0, dims[axis]) for axis in range(len(dims))]
    entries = entries.at[tuple(spot)].set(least)
    longest = dims.index(max(dims))
    spot[longest] = (spot[longest] + 1) % dims[longest]
    return entries.at[tuple(spot)].set(high)


def block_scale(key, shape, split, low, high):
    def one(axis_at, shards_of):
        steps = jax.random.uniform(jax.random.fold_in(jax.random.fold_in(key, 6), axis_at), (shards_of,), jnp.float32, low / len(split), high / len(split))
        return jnp.repeat(jnp.exp(steps), shape[axis_at] // shards_of).reshape((-1,) + (1,) * (len(shape) - axis_at - 1))

    gain = one(*split[0])
    for cut in split[1:]:
        gain = gain * one(*cut)
    return gain


def setup_inputs(seed: int = 0) -> dict:
    key_of = jax.random.split(jax.random.key(seed), 6)
    head_old = jnp.clip(-0.12 + 0.09999999776482582 * jax.random.uniform(key_of[0], (NZ, NX, NY), jnp.float32) ** block_scale(key_of[0], (NZ, NX, NY), ((0, 4), (1, 8)), -0.2, 0.2), -0.12, -0.02)
    soil_type = plant(jax.random.randint(key_of[1], (NZ, NX, NY), 0, NSOIL), jax.random.fold_in(key_of[1], 1), 0, NSOIL - 1).astype(jnp.int32)
    soil_table = draw_soil_table(jax.random.fold_in(key_of[5], 71), 0)
    land_mask = plant((jax.random.randint(key_of[3], (NX, NY), 0, 4) < 3).astype(jnp.int32), jax.random.fold_in(key_of[3], 1), 0, 1)
    sun_bin = plant(jax.random.randint(key_of[4], (NX, NY), 0, 24), jax.random.fold_in(key_of[4], 1), 0, 23).astype(jnp.int32)
    return {"head_old": head_old, "soil_type": soil_type, "soil_table": soil_table, "land_mask": land_mask, "sun_bin": sun_bin}


dt_step = 20.0
et_peak = 0.008
gravity = 0.1
root_decay = 3.0

def soil_state(pressure, params):
    water_resid, water_sat, alpha_coef, shape_coef, k_sat = params
    expon_m = 1.0 - 1.0 / shape_coef
    scaled = jnp.abs(alpha_coef * pressure)
    power_p = jnp.power(scaled, shape_coef)
    base_one = 1.0 + power_p
    saturation = jnp.power(base_one, -expon_m)
    slope = expon_m * shape_coef * alpha_coef * jnp.power(scaled, shape_coef - 1.0) * jnp.power(base_one, -expon_m - 1.0)
    content = water_resid + (water_sat - water_resid) * saturation
    capacity = (water_sat - water_resid) * slope
    relative = jnp.sqrt(saturation) * jnp.square(1.0 - jnp.power(power_p / base_one, expon_m))
    conduct = k_sat * relative
    return (saturation, slope, content, capacity, conduct)

def pair_sum(tensor, position):
    extent = tensor.shape
    split_shape = extent[:position] + (extent[position] // 2, 2) + extent[position + 1:]
    return lax.optimization_barrier(jnp.sum(tensor.reshape(split_shape), axis=position + 1))

def make_stencil(storage, face_across, face_vertical, face_along):
    diagonal = storage + face_across[:, :-1, :] + face_across[:, 1:, :] + face_vertical[:-1] + face_vertical[1:]
    diagonal = diagonal + face_along[..., :-1] + face_along[..., 1:]
    return (storage, face_across, face_vertical, face_along, diagonal)

def coarsen(stencil):
    storage, face_across, face_vertical, face_along, diagonal = stencil
    store_new = pair_sum(pair_sum(pair_sum(storage, 0), 1), 2)
    across_new = pair_sum(pair_sum(face_across[:, ::2, :], 0), 2)
    vertical_new = pair_sum(pair_sum(face_vertical[::2], 1), 2)
    along_new = pair_sum(pair_sum(face_along[..., ::2], 0), 1)
    return make_stencil(store_new, across_new, vertical_new, along_new)

def restrict(residual):
    return pair_sum(pair_sum(pair_sum(residual, 0), 1), 2)

def prolong(coarse):
    return jnp.repeat(jnp.repeat(jnp.repeat(coarse, 2, axis=0), 2, axis=1), 2, axis=2)

def parity(extent):
    layer_count, row_count, col_count = extent
    return jnp.remainder(jnp.arange(layer_count)[:, None, None] + jnp.arange(row_count)[None, :, None] + jnp.arange(col_count)[None, None, :], 2)

def neighbour_sum(field, stencil):
    storage, face_across, face_vertical, face_along, diagonal = stencil
    pad_across = jnp.pad(field, ((0, 0), (1, 1), (0, 0)))
    pad_vertical = jnp.pad(field, ((1, 1), (0, 0), (0, 0)))
    pad_along = jnp.pad(field, ((0, 0), (0, 0), (1, 1)))
    total = face_across[:, :-1, :] * pad_across[:, :-2, :] + face_across[:, 1:, :] * pad_across[:, 2:, :]
    total = total + face_vertical[:-1] * pad_vertical[:-2] + face_vertical[1:] * pad_vertical[2:]
    total = total + face_along[..., :-1] * pad_along[..., :-2] + face_along[..., 1:] * pad_along[..., 2:]
    return total

def solve_blocks(block_rhs, block_store, block_across, block_vertical, slab_count):
    across_up = jnp.concatenate([block_across[slab_count:], jnp.zeros((slab_count,), block_across.dtype)])
    vertical_up = jnp.concatenate([block_vertical[1:], jnp.zeros((1,), block_vertical.dtype)])
    diagonal = block_store + block_across + across_up + block_vertical + vertical_up
    matrix = jnp.diag(diagonal) - jnp.diag(block_across[slab_count:], slab_count) - jnp.diag(block_across[slab_count:], -slab_count)
    matrix = matrix - jnp.diag(block_vertical[1:], 1) - jnp.diag(block_vertical[1:], -1)
    factor = jnp.linalg.cholesky(matrix)
    return jax.scipy.linalg.cho_solve((factor, True), block_rhs)

def block_correction(residual, stencil):
    storage, face_across, face_vertical, face_along, diagonal = stencil
    layer_count, row_count, col_count = residual.shape
    block_layers = layer_count // N_GZ
    block_rows = row_count // N_XY

    def blocks(tensor):
        return lax.optimization_barrier(jnp.sum(tensor.reshape(N_GZ, block_layers, N_XY, block_rows, col_count), axis=(1, 3, 4))).T.reshape(-1)
    block_rhs = blocks(residual)
    block_store = blocks(storage)
    block_across = lax.optimization_barrier(jnp.sum(face_across[:, 0:row_count:block_rows, :].reshape(N_GZ, block_layers, N_XY, col_count), axis=(1, 3))).T.reshape(-1)
    block_vertical = lax.optimization_barrier(jnp.sum(face_vertical[0:layer_count:block_layers].reshape(N_GZ, N_XY, block_rows, col_count), axis=(2, 3))).T.reshape(-1)
    answer = solve_blocks(block_rhs, block_store, block_across, block_vertical, N_GZ)
    grid_values = answer.reshape(N_XY, N_GZ).T
    spread = jnp.repeat(jnp.repeat(grid_values, block_layers, axis=0), block_rows, axis=1)
    return spread[:, :, None]

def vcycle(stencils, source, level_index):
    stencil = stencils[level_index]
    diagonal = stencil[4]
    colour = parity(source.shape)
    correction = jnp.where(colour == 0, source / diagonal, 0.0)
    correction = jnp.where(colour == 1, (source + neighbour_sum(correction, stencil)) / diagonal, correction)
    residual = source - (diagonal * correction - neighbour_sum(correction, stencil))
    if level_index + 1 < len(stencils):
        correction = correction + prolong(vcycle(stencils, restrict(residual), level_index + 1))
    else:
        correction = correction + block_correction(residual, stencil)
    correction = jnp.where(colour == 0, (source + neighbour_sum(correction, stencil)) / diagonal, correction)
    correction = jnp.where(colour == 1, (source + neighbour_sum(correction, stencil)) / diagonal, correction)
    return correction

def reference(head_old, soil_type, soil_table, land_mask, sun_bin):
    params = [soil_table[position][soil_type] for position in range(5)]
    layer_depth = jnp.arange(NZ).astype(jnp.float32)
    root_share = jnp.exp(-root_decay * layer_depth / NZ)
    sun_share = jnp.maximum(0.0, jnp.sin(math.pi * (sun_bin.astype(jnp.float32) - 6.0) / 12.0))
    forcing = et_peak * sun_share * land_mask.astype(jnp.float32)
    sink_rate = forcing[None] * root_share[:, None, None]
    content_old = soil_state(head_old, params)[2]
    pressure = head_old
    for newton_step in range(NEWTON):
        saturation, slope, content, capacity, conduct = soil_state(pressure, params)
        zero_x = jnp.zeros_like(conduct[:, :1, :])
        face_across = jnp.concatenate([zero_x, 0.5 * (conduct[:, :-1, :] + conduct[:, 1:, :]), zero_x], axis=1)
        zero_z = jnp.zeros_like(conduct[:1])
        face_vertical = jnp.concatenate([zero_z, 0.5 * (conduct[:-1] + conduct[1:]), zero_z], axis=0)
        zero_y = jnp.zeros_like(conduct[..., :1])
        face_along = jnp.concatenate([zero_y, 0.5 * (conduct[..., :-1] + conduct[..., 1:]), zero_y], axis=2)
        pad_across = jnp.pad(pressure, ((0, 0), (1, 1), (0, 0)))
        flux_across = face_across * (pad_across[:, :-1, :] - pad_across[:, 1:, :])
        potential = pressure - gravity * layer_depth[:, None, None]
        pad_vertical = jnp.pad(potential, ((1, 1), (0, 0), (0, 0)))
        flux_vertical = face_vertical * (pad_vertical[:-1] - pad_vertical[1:])
        pad_along = jnp.pad(pressure, ((0, 0), (0, 0), (1, 1)))
        flux_along = face_along * (pad_along[..., :-1] - pad_along[..., 1:])
        residual = (content - content_old) / dt_step + sink_rate * saturation
        residual = residual + (flux_across[:, 1:, :] - flux_across[:, :-1, :])
        residual = residual + (flux_along[..., 1:] - flux_along[..., :-1])
        residual = residual + (flux_vertical[1:] - flux_vertical[:-1])
        storage = capacity / dt_step + sink_rate * slope
        stencils = [make_stencil(storage, face_across, face_vertical, face_along)]
        for coarse_step in range(LEVELS - 1):
            stencils.append(coarsen(stencils[-1]))
        pressure = pressure + vcycle(stencils, -residual, 0)
    return pressure
```

```python
import functools
import math

import jax
import jax.numpy as jnp
from jax import lax
from jax.experimental import pallas as pl
from jax.experimental.pallas import tpu as pltpu
from jax.sharding import PartitionSpec as P

DT = 20.0
ET_PEAK = 0.008
GRAVITY = 0.1
ROOT_DECAY = 3.0
HI = lax.Precision.HIGHEST


def roll(value, shift, axis):
    return pltpu.roll(value, shift % value.shape[axis], axis)


def spread_pairs(value, low, step, axis):
    return value + jnp.where(low, roll(value, -step, axis), roll(value, step, axis))


def neighbour_sum(e, below, above, fx, fy, fz, fz_up, step):
    total = fx * roll(e, step, 0) + roll(fx * e, -step, 0)
    total = total + (fy * roll(e, step, 1) + roll(fy * e, -step, 1))
    return total + (fz * below + fz_up * above)


def look_up(table, row, index):
    picked = jnp.broadcast_to(table[row : row + 1, :], (8, 128))
    rows = []
    for r in range(0, index.shape[0], 8):
        cols = []
        for c in range(0, index.shape[1], 128):
            at = index[r : r + 8, c : c + 128]
            cols.append(jnp.take_along_axis(picked, at, axis=1, mode="promise_in_bounds"))
        rows.append(jnp.concatenate(cols, axis=1))
    return jnp.concatenate(rows, axis=0)


def down_kernel(first, slabs, strips, zl, xl, *refs):
    where_ref, table_ref = refs[0], refs[1]
    refs = refs[2:]
    state_refs, refs = refs[:9], refs[9:]
    if first:
        head_refs = state_refs
        sat_old_ref = None
    else:
        head_refs, refs = refs[:9], refs[9:]
        sat_old_ref, refs = refs[0], refs[1:]
    payload_ref, refs = refs[0], refs[1:]
    outs0, refs = refs[:6], refs[6:]
    outs1, refs = refs[:5], refs[5:]
    head_out = None
    if first:
        head_out, refs = refs[0], refs[1:]
    head, cond, stor, grow, fx, fy, fz, src, inv, err = refs[:10]
    src1, stor1, fx1, fy1, fz1, inv1, err1, rows2 = refs[10:]

    strip, slab = where_ref[0], where_ref[1]
    zw, xw = 3 * zl, 3 * xl
    ny = head.shape[2]
    shape = (xw, ny)
    xi = lax.broadcasted_iota(jnp.int32, shape, 0)
    yi = lax.broadcasted_iota(jnp.int32, shape, 1)
    parity0 = (xi + yi) & 1
    parity1 = ((xi >> 1) + (yi >> 1)) & 1
    x_low, y_low = (xi & 1) == 0, (yi & 1) == 0
    x_low2, y_low2 = (xi & 2) == 0, (yi & 2) == 0
    edge_x = jnp.logical_or(
        jnp.logical_and(xi == xl, strip == 0), jnp.logical_and(xi == 2 * xl, strip == strips - 1)
    )
    edge_y = yi == 0

    def edge_z(z, width):
        return jnp.logical_or(
            jnp.logical_and(z == width, slab == 0),
            jnp.logical_and(z == 2 * width, slab == slabs - 1),
        )

    forcing = jnp.concatenate([r[2 * zl] for r in state_refs[3:6]], axis=0)
    table = table_ref[...]

    for zb in range(3):

        def soil_step(i, carry, zb=zb):
            z = zb * zl + i
            soil = jnp.concatenate([r[zl + i] for r in state_refs[3 * zb : 3 * zb + 3]], axis=0)
            p = jnp.concatenate([r[i] for r in head_refs[3 * zb : 3 * zb + 3]], axis=0)
            soil = soil.astype(jnp.int32)
            dtheta, alpha, shape_n, k_sat, expon_m = (look_up(table, k, soil) for k in range(5))
            layer = (slab * zl - zl + z).astype(jnp.float32)
            depth = jnp.full((1, ny), layer, jnp.float32)
            sink = forcing * jnp.exp(-ROOT_DECAY * depth / (slabs * zl))
            log_s = jnp.log(jnp.abs(alpha * p))
            log_p = shape_n * log_s
            log_b = jnp.log(1.0 + jnp.exp(log_p))
            root = jnp.exp(-0.5 * expon_m * log_b)
            sat = root * root
            slope = expon_m * shape_n * alpha * sat * jnp.exp((shape_n - 1.0) * log_s - log_b)
            cond[z] = k_sat * root * jnp.square(1.0 - jnp.exp(expon_m * (log_p - log_b)))
            stor[z] = slope * (dtheta / DT + sink)
            g = sink * sat
            if first:
                head_out[z] = sat
            else:
                g = g + dtheta * (sat - sat_old_ref[z]) / DT
            grow[z] = g
            head[z] = p
            return carry

        lax.fori_loop(0, zl, soil_step, 0)

    def face_z(z):
        both = 0.5 * (cond[jnp.maximum(z - 1, 0)] + cond[jnp.minimum(z, zw - 1)])
        closed = jnp.logical_or(edge_z(z, zl), jnp.logical_or(z == 0, z == zw))
        return both * jnp.where(closed, 0.0, 1.0)

    fz[0] = jnp.zeros(shape, jnp.float32)

    def face_step(z, carry):
        c, p = cond[z], head[z]
        across = jnp.where(edge_x, 0.0, 0.5 * (c + roll(c, 1, 0)))
        along = jnp.where(edge_y, 0.0, 0.5 * (c + roll(c, 1, 1)))
        low, high = fz[z], face_z(z + 1)
        flux_x = across * (roll(p, 1, 0) - p)
        flux_y = along * (roll(p, 1, 1) - p)
        p_low, p_high = head[jnp.maximum(z - 1, 0)], head[jnp.minimum(z + 1, zw - 1)]
        flux_low = low * (p_low - p + GRAVITY)
        flux_high = high * (p - p_high + GRAVITY)
        source = (flux_x - roll(flux_x, -1, 0)) + (flux_y - roll(flux_y, -1, 1))
        source = source + (flux_low - flux_high) - grow[z]
        diagonal = stor[z] + (across + roll(across, -1, 0)) + (along + roll(along, -1, 1))
        inverse = 1.0 / (diagonal + (low + high))
        fx[z], fy[z], fz[z + 1] = across, along, high
        src[z], inv[z] = source, inverse
        err[z] = jnp.where(parity0 == (z & 1), source * inverse, 0.0)
        return carry

    lax.fori_loop(0, zw, face_step, 0)

    def sum0(z):
        return neighbour_sum(
            err[z],
            err[jnp.maximum(z - 1, 0)],
            err[jnp.minimum(z + 1, zw - 1)],
            fx[z],
            fy[z],
            fz[z],
            fz[z + 1],
            1,
        )

    def smooth_step(z, carry):
        updated = (src[z] + sum0(z)) * inv[z]
        err[z] = jnp.where(parity0 == (z & 1), err[z], updated)
        return carry

    lax.fori_loop(1, zw - 1, smooth_step, 0)

    def coarse_step(k, carry):
        za, zb = 2 * k, 2 * k + 1
        resid = jnp.where(parity0 == 0, sum0(za), sum0(zb))
        src1[k] = spread_pairs(spread_pairs(resid, x_low, 1, 0), y_low, 1, 1)
        stor1[k] = spread_pairs(spread_pairs(stor[za] + stor[zb], x_low, 1, 0), y_low, 1, 1)
        across = spread_pairs(fx[za] + fx[zb], y_low, 1, 1)
        fx1[k] = jnp.where(x_low, across, roll(across, 1, 0))
        along = spread_pairs(fy[za] + fy[zb], x_low, 1, 0)
        fy1[k] = jnp.where(y_low, along, roll(along, 1, 1))
        fz1[k] = spread_pairs(spread_pairs(fz[za], x_low, 1, 0), y_low, 1, 1)
        return carry

    lax.fori_loop(1, zw // 2 - 1, coarse_step, 0)

    def first1(k, carry):
        across, along = fx1[k], fy1[k]
        diagonal = stor1[k] + (across + roll(across, -2, 0)) + (along + roll(along, -2, 1))
        inverse = 1.0 / (diagonal + (fz1[k] + fz1[k + 1]))
        inv1[k] = inverse
        err1[k] = jnp.where(parity1 == (k & 1), src1[k] * inverse, 0.0)
        return carry

    low1, high1 = zl // 2 - 2, zl + 2
    lax.fori_loop(low1, high1, first1, 0)

    def sum1(k):
        return neighbour_sum(
            err1[k], err1[k - 1], err1[k + 1], fx1[k], fy1[k], fz1[k], fz1[k + 1], 2
        )

    def second1(k, carry):
        updated = (src1[k] + sum1(k)) * inv1[k]
        err1[k] = jnp.where(parity1 == (k & 1), err1[k], updated)
        return carry

    lax.fori_loop(low1 + 1, high1 - 1, second1, 0)

    rows2[...] = jnp.zeros(rows2.shape, jnp.float32)
    own1 = zl // 2
    for k2 in range(zl // 4):
        ka, kb = own1 + 2 * k2, own1 + 2 * k2 + 1
        resid = jnp.where(parity1 == 0, sum1(ka), sum1(kb))
        terms = (
            spread_pairs(spread_pairs(resid, x_low2, 2, 0), y_low2, 2, 1),
            spread_pairs(spread_pairs(stor1[ka] + stor1[kb], x_low2, 2, 0), y_low2, 2, 1),
            spread_pairs(fx1[ka] + fx1[kb], y_low2, 2, 1),
            spread_pairs(fy1[ka] + fy1[kb], x_low2, 2, 0),
            spread_pairs(spread_pairs(fz1[ka], x_low2, 2, 0), y_low2, 2, 1),
        )
        for t, term in enumerate(terms):
            for x2 in range(xl // 4):
                at = (t * (xl // 4) + x2) * (zl // 4) + k2
                x = xl + 4 * x2
                rows2[at : at + 1, :] = term[x : x + 1, :]
    pick_shape = (ny, ny // 4)
    pick = lax.broadcasted_iota(jnp.int32, pick_shape, 0) == 4 * lax.broadcasted_iota(
        jnp.int32, pick_shape, 1
    )
    payload_ref[0 : rows2.shape[0], :] = jnp.dot(
        rows2[...], jnp.where(pick, 1.0, 0.0), precision=HI, preferred_element_type=jnp.float32
    )
    own = slice(xl, 2 * xl)
    here = [err1[own1 + k][own] for k in range(4)]
    xo, yo = x_low[own], y_low[own]
    plane = jnp.where(xo, jnp.where(yo, here[0], here[1]), jnp.where(yo, here[2], here[3]))
    base = rows2.shape[0]
    for c in range(ny // 128):
        payload_ref[base + 8 * c : base + 8 * c + 8, :] = plane[:, 128 * c : 128 * c + 128]

    def keep0(i, carry):
        for out, ref in zip(outs0, (err, src, inv, fx, fy, fz)):
            out[i] = ref[zl - 2 + i]
        return carry

    lax.fori_loop(0, zl + 4, keep0, 0)

    def keep1(i, carry):
        for out, ref in zip(outs1, (src1, inv1, fx1, fy1, fz1)):
            out[i] = ref[zl // 2 - 2 + i]
        return carry

    lax.fori_loop(0, zl // 2 + 5, keep1, 0)


def solve_blocks(rhs, store, across, vertical, scratch, answer):
    count = rhs.shape[0]
    sub = lax.broadcasted_iota(jnp.int32, (8, 128), 0)
    lane = lax.broadcasted_iota(jnp.int32, (8, 128), 1)
    real = (sub & 1) == 0
    same = lane == sub

    def forward(b, before):
        here_x = jnp.where(real, across[b], 0.0)
        next_x = jnp.where(real, across[b + 1], 0.0)
        low = jnp.where(real, vertical[b], 0.0)
        high = roll(low, -2, 0)
        diagonal = jnp.where(real, store[b] + here_x + next_x + low + high, 1.0)
        m = jnp.where(same, diagonal, 0.0)
        m = m - jnp.where(lane == sub - 2, low, 0.0) - jnp.where(lane == sub + 2, high, 0.0)
        m = m - jnp.where(lane == sub + 8, next_x, 0.0)
        m = m + jnp.where(jnp.logical_and(lane == 16, real), rhs[b], 0.0)
        carried = jnp.where(lane < 8, roll(before, -8, 1), jnp.where(lane == 16, before, 0.0))
        m = m + here_x * carried
        for z in range(0, 8, 2):
            row = m[z : z + 1, :]
            row = row / row[:, z : z + 1]
            m = jnp.where(sub == z, row, m - m[:, z : z + 1] * row)
        scratch[b] = m
        return m

    lax.fori_loop(0, count, forward, jnp.zeros((8, 128), jnp.float32))

    def backward(i, above):
        b = count - 1 - i
        m = scratch[b]
        row = jnp.sum(jnp.where(lane == sub + 8, above, 0.0), axis=0, keepdims=True)
        mask = jnp.logical_and(lane >= 8, lane < 16)
        taken = jnp.where(lane == 16, m, 0.0) - jnp.where(mask, m * row, 0.0)
        value = jnp.broadcast_to(jnp.sum(taken, axis=1, keepdims=True), (8, 128))
        answer[b] = jnp.where(real, value, roll(value, 1, 0))
        return value

    lax.fori_loop(0, count, backward, jnp.zeros((8, 128), jnp.float32))


def up_kernel(slabs, strips, zl, xl, counts, *refs):
    where_ref, refs = refs[0], refs[1:]
    pieces, refs = refs[: len(counts)], refs[len(counts) :]
    near, refs = refs[:3], refs[3:]
    e0_in, src0, inv0, fx0, fy0, fz0 = refs[:6]
    src1, inv1, fx1, fy1, fz1 = refs[6:11]
    head_ref, out_ref = refs[11], refs[12]
    a2, block, answer, e2, picked, wide, e1, e0 = refs[13:]
    strip, slab = where_ref[0], where_ref[1]
    x2, z2 = xl // 4, zl // 4
    rows2 = strips * x2
    ny = head_ref.shape[2]

    index = 0
    for ref, count in zip(pieces, counts):
        for j in range(count):
            at = jnp.bitwise_xor(strip, index)
            for g in range(slabs):
                piece = ref[j, jnp.bitwise_xor(slab, g)]
                for t in range(5):
                    for x in range(x2):
                        k = (t * x2 + x) * z2
                        a2[t, at * x2 + x, g * z2 : g * z2 + z2, :] = piece[k : k + z2, :]
            index += 1

    shape = (rows2, 8, 128)
    source, store, fx, fy, fz = (a2[t] for t in range(5))

    def shift_x(v, step):
        if step > 0:
            return jnp.concatenate([jnp.zeros_like(v[:1]), v[:-1]], axis=0)
        return jnp.concatenate([v[1:], jnp.zeros_like(v[:1])], axis=0)

    def along(v, step, axis):
        return pltpu.roll(v, step % v.shape[axis], axis)

    fx_up, fy_up, fz_up = shift_x(fx, -1), along(fy, -1, 2), along(fz, -1, 1)
    inverse = 1.0 / (store + (fx + fx_up) + (fy + fy_up) + (fz + fz_up))
    parity = (
        lax.broadcasted_iota(jnp.int32, shape, 0)
        + lax.broadcasted_iota(jnp.int32, shape, 1)
        + lax.broadcasted_iota(jnp.int32, shape, 2)
    ) & 1
    even = parity == 0

    def sum2(e):
        total = fx * shift_x(e, 1) + fx_up * shift_x(e, -1)
        total = total + (fy * along(e, 1, 2) + fy_up * along(e, -1, 2))
        return total + (fz * along(e, 1, 1) + fz_up * along(e, -1, 1))

    e = jnp.where(even, source * inverse, 0.0)
    e = jnp.where(even, e, (source + sum2(e)) * inverse)
    resid = jnp.where(even, sum2(e), 0.0)

    def blocks(v, both_rows, both_layers):
        v = v.reshape(strips, x2, 8, 128)
        v = v[:, 0] + v[:, 1] if both_rows else v[:, 0]
        v = jnp.sum(v, axis=2, keepdims=True)
        v = jnp.broadcast_to(v, (strips, 8, 128))
        return v + along(v, -1, 1) if both_layers else v

    block[0, 0:strips] = blocks(resid, True, True)
    block[1, 0:strips] = blocks(store, True, True)
    block[2, 0:strips] = blocks(fx, False, True)
    block[2, strips] = jnp.zeros((8, 128), jnp.float32)
    block[3, 0:strips] = blocks(fz, True, False)
    solve_blocks(
        block.at[0, 0:strips], block.at[1], block.at[2], block.at[3], block.at[4], answer
    )
    add = jnp.broadcast_to(answer[...][:, None], (strips, x2, 8, 128)).reshape(shape)
    e = e + add
    e = jnp.where(even, (source + sum2(e)) * inverse, e)
    e = jnp.where(even, e, (source + sum2(e)) * inverse)
    e2[...] = jnp.zeros(e2.shape, jnp.float32)
    e2[x2 : x2 + rows2, 8:16, :] = e

    picked[...] = jnp.zeros(picked.shape, jnp.float32)
    for z in range(3 * z2):
        for x in range(3 * x2):
            at = z * 3 * x2 + x
            picked[at : at + 1, :] = e2[
                strip * x2 + x, pl.ds(8 - z2 + slab * z2 + z, 1), :
            ]
    spread_shape = (ny // 4, ny)
    spread = lax.broadcasted_iota(jnp.int32, spread_shape, 0) == (
        lax.broadcasted_iota(jnp.int32, spread_shape, 1) >> 2
    )
    wide[...] = jnp.dot(
        picked[...], jnp.where(spread, 1.0, 0.0), precision=HI, preferred_element_type=jnp.float32
    )

    zl1 = zl // 2
    small = (xl, ny)
    xo = (lax.broadcasted_iota(jnp.int32, small, 0) & 1) == 0
    yo = (lax.broadcasted_iota(jnp.int32, small, 1) & 1) == 0
    for zb in range(3):
        g = slab + (zb - 1)
        inside = jnp.logical_and(g >= 0, g < slabs)
        m = jnp.bitwise_xor(slab, jnp.clip(g, 0, slabs - 1))
        keep = jnp.where(inside, 1.0, 0.0)
        for xb in range(3):
            tile = near[xb][m]
            plane = jnp.concatenate(
                [tile[8 * c : 8 * c + 8, :] for c in range(ny // 128)], axis=1
            )
            plane = plane * keep
            for k in range(4):
                xk, yk = k // 2, k % 2
                v = jnp.where(jnp.logical_and(xo == (xk == 0), yo == (yk == 0)), plane, 0.0)
                v = v + roll(v, 1 if xk == 0 else -1, 0)
                v = v + roll(v, 1 if yk == 0 else -1, 1)
                for h in range(xl // 4):
                    row = ((zb * zl1 + k) // 2) * 3 * x2 + xb * x2 + h
                    e1[zb * zl1 + k, xb * xl + 4 * h : xb * xl + 4 * h + 4, :] = (
                        v[4 * h : 4 * h + 4, :] + wide[row : row + 1, :]
                    )
    window = (3 * xl, ny)
    xi = lax.broadcasted_iota(jnp.int32, window, 0)
    yi = lax.broadcasted_iota(jnp.int32, window, 1)
    parity0 = (xi + yi) & 1
    parity1 = ((xi >> 1) + (yi >> 1)) & 1

    def level1(k, colour):
        i = k - (zl1 - 2)
        total = neighbour_sum(
            e1[k], e1[k - 1], e1[k + 1], fx1[i], fy1[i], fz1[i], fz1[i + 1], 2
        )
        updated = (src1[i] + total) * inv1[i]
        e1[k] = jnp.where(parity1 == ((k + colour) & 1), updated, e1[k])

    def up1(colour, reach):
        def step(k, carry):
            level1(k, colour)
            return carry

        lax.fori_loop(zl1 - reach, 2 * zl1 + reach, step, 0)

    up1(0, 2)
    up1(1, 1)

    def join(i, carry):
        e0[i] = e0_in[i] + e1[(zl - 2 + i) // 2]
        return carry

    lax.fori_loop(0, zl + 4, join, 0)

    def up0(colour, reach):
        def step(i, carry):
            total = neighbour_sum(
                e0[i], e0[i - 1], e0[i + 1], fx0[i], fy0[i], fz0[i], fz0[i + 1], 1
            )
            updated = (src0[i] + total) * inv0[i]
            e0[i] = jnp.where(parity0 == ((i + colour) & 1), updated, e0[i])
            return carry

        lax.fori_loop(2 - reach, zl + 2 + reach, step, 0)

    up0(0, 1)
    up0(1, 0)
    for z in range(zl):
        out_ref[z] = head_ref[z] + e0[z + 2][xl : 2 * xl]


VMEM = pl.BlockSpec(memory_space=pltpu.VMEM)
SMEM = pl.BlockSpec(memory_space=pltpu.SMEM)


def f32(*shape):
    return jax.ShapeDtypeStruct(shape, jnp.float32)


def down(first, slabs, strips, zl, xl, ny, where, table, state, head=None, sat_old=None):
    zw, xw = 3 * zl, 3 * xl
    rows2 = 5 * (xl // 4) * (zl // 4)
    rows2 = -(-rows2 // 8) * 8
    out_shape = [f32(rows2 + 8 * ny // 128, 128)]
    out_shape += [f32(zl + 4, xw, ny)] * 6 + [f32(zl // 2 + 5, xw, ny)] * 5
    operands = [where, table, *state]
    if first:
        out_shape.append(f32(zw, xw, ny))
    else:
        operands += [*head, sat_old]
    full, half = pltpu.VMEM((zw, xw, ny), jnp.float32), pltpu.VMEM((zw // 2, xw, ny), jnp.float32)
    tall = pltpu.VMEM((zw + 1, xw, ny), jnp.float32)
    return pl.pallas_call(
        functools.partial(down_kernel, first, slabs, strips, zl, xl),
        out_shape=out_shape,
        in_specs=[SMEM] + [VMEM] * (len(operands) - 1),
        out_specs=[VMEM] * len(out_shape),
        scratch_shapes=[full] * 6 + [tall] + [full] * 3 + [half] * 7
        + [pltpu.VMEM((rows2, ny), jnp.float32)],
        compiler_params=pltpu.CompilerParams(vmem_limit_bytes=44 * 1024 * 1024),
    )(*operands)


def up(slabs, strips, zl, xl, ny, where, pieces, near, kept, head):
    x2, z2 = xl // 4, zl // 4
    counts = [p.shape[0] for p in pieces]
    operands = [where, *pieces, *near, *kept, head]
    n = -(-9 * x2 * z2 // 8) * 8
    scratch = [
        pltpu.VMEM((5, strips * x2, 8, 128), jnp.float32),
        pltpu.VMEM((5, strips + 1, 8, 128), jnp.float32),
        pltpu.VMEM((strips, 8, 128), jnp.float32),
        pltpu.VMEM(((strips + 2) * x2, 24, 128), jnp.float32),
        pltpu.VMEM((n, ny // 4), jnp.float32),
        pltpu.VMEM((n, ny), jnp.float32),
        pltpu.VMEM((3 * zl // 2, 3 * xl, ny), jnp.float32),
        pltpu.VMEM((zl + 4, 3 * xl, ny), jnp.float32),
    ]
    return pl.pallas_call(
        functools.partial(up_kernel, slabs, strips, zl, xl, counts),
        out_shape=f32(zl, xl, ny),
        in_specs=[SMEM] + [VMEM] * (len(operands) - 1),
        out_specs=VMEM,
        scratch_shapes=scratch,
        compiler_params=pltpu.CompilerParams(vmem_limit_bytes=44 * 1024 * 1024),
    )(*operands)


def shifted(x, axis, step):
    size = lax.axis_size(axis)
    pairs = [(i, i + step) for i in range(size) if 0 <= i + step < size]
    return lax.ppermute(x, axis, pairs)


def swapped(x, axis, mask):
    return lax.ppermute(x, axis, [(i, i ^ mask) for i in range(lax.axis_size(axis))])


def neighbourhood(x):
    row = [shifted(x, "xy", 1), x, shifted(x, "xy", -1)]
    return (
        [shifted(v, "gz", 1) for v in row] + row + [shifted(v, "gz", -1) for v in row]
    )


def gather_strips(x):
    size = lax.axis_size("xy")
    x = x[None]
    if size == 8:
        pair = jnp.concatenate([x, swapped(x, "xy", 1)])
        return [pair] + [swapped(pair, "xy", m) for m in (2, 4, 6)]
    mask = 1
    while mask < size:
        x = jnp.concatenate([x, swapped(x, "xy", mask)])
        mask *= 2
    return [x]


def per_device(head_old, soil_type, soil_table, land_mask, sun_bin):
    zl, xl, ny = head_old.shape
    strips, slabs = lax.axis_size("xy"), lax.axis_size("gz")
    where = jnp.stack([lax.axis_index("xy"), lax.axis_index("gz")]).astype(jnp.int32)
    resid, sat, alpha, shape_n, k_sat = soil_table
    table = jnp.stack([sat - resid, alpha, shape_n, k_sat, 1.0 - 1.0 / shape_n])
    table = jnp.pad(table, ((0, 3), (0, 128 - table.shape[1])))
    sun_share = jnp.maximum(0.0, jnp.sin(math.pi * (sun_bin.astype(jnp.float32) - 6.0) / 12.0))
    forcing = ET_PEAK * sun_share * land_mask.astype(jnp.float32)
    own = jnp.concatenate([head_old, soil_type.astype(jnp.float32), forcing[None]])
    state = neighbourhood(own)
    sizes = (slabs, strips, zl, xl, ny)
    base = -(-5 * (xl // 4) * (zl // 4) // 8) * 8

    def finish(payload, kept, head):
        slab = [payload] + [swapped(payload, "gz", m) for m in range(1, slabs)]
        equations = jnp.stack([p[:base] for p in slab])
        corrections = jnp.stack([p[base:] for p in slab])
        pieces = gather_strips(equations)
        near = [shifted(corrections, "xy", 1), corrections, shifted(corrections, "xy", -1)]
        return up(*sizes, where, pieces, near, kept, head)

    payload, *kept, sat_old = down(True, *sizes, where, table, state)
    head = finish(payload, kept, head_old)
    payload, *kept = down(False, *sizes, where, table, state, neighbourhood(head), sat_old)
    return finish(payload, kept, head)


def solution(mesh):
    in_specs = (P("gz", "xy", None), P("gz", "xy", None), P(), P("xy", None), P("xy", None))
    out_specs = P("gz", "xy", None)
    return jax.shard_map(
        per_device, mesh=mesh, in_specs=in_specs, out_specs=out_specs, check_vma=False
    )
```

```python
import functools
import math

import jax
import jax.numpy as jnp
from jax import lax
from jax.experimental import pallas as pl
from jax.experimental.pallas import tpu as pltpu
from jax.sharding import PartitionSpec as P

DT = 20.0
ET_PEAK = 0.008
GRAVITY = 0.1
ROOT_DECAY = 3.0
HI = lax.Precision.HIGHEST


def roll(value, shift, axis):
    return pltpu.roll(value, shift % value.shape[axis], axis)


def place(which, index):
    if which == 0:
        return 1
    odd = index & 1
    return 2 - 2 * odd if which == 1 else 2 * odd


def spread_pairs(value, low, step, axis):
    return value + jnp.where(low, roll(value, -step, axis), roll(value, step, axis))


def neighbour_sum(e, below, above, fx, fy, fz, fz_up, step):
    total = fx * roll(e, step, 0) + roll(fx * e, -step, 0)
    total = total + (fy * roll(e, step, 1) + roll(fy * e, -step, 1))
    return total + (fz * below + fz_up * above)


def look_up(table, row, index):
    picked = jnp.broadcast_to(table[row : row + 1, :], (8, 128))
    rows = []
    for r in range(0, index.shape[0], 8):
        cols = []
        for c in range(0, index.shape[1], 128):
            at = index[r : r + 8, c : c + 128]
            cols.append(jnp.take_along_axis(picked, at, axis=1, mode="promise_in_bounds"))
        rows.append(jnp.concatenate(cols, axis=1))
    return jnp.concatenate(rows, axis=0)


def down_kernel(first, slabs, strips, zl, xl, *refs):
    where_ref, table_ref = refs[0], refs[1]
    refs = refs[2:]
    state_refs, refs = refs[:9], refs[9:]
    if first:
        head_refs = state_refs
    else:
        head_refs, refs = refs[:9], refs[9:]
        sat_old_ref, refs = refs[0], refs[1:]
    payload_ref, refs = refs[0], refs[1:]
    outs0, refs = refs[:6], refs[6:]
    outs1, refs = refs[:5], refs[5:]
    if first:
        sat_out, refs = refs[0], refs[1:]
    head, cond, stor, grow, fx, fy, fz, src, inv, err = refs[:10]
    src1, stor1, fx1, fy1, fz1, inv1, err1, rows2 = refs[10:]

    strip, slab = where_ref[0], where_ref[1]
    zw, xw = 3 * zl, 3 * xl
    ny = head.shape[3]
    shape = (xw, ny)

    def slab_of(ref, z):
        return ref[z].reshape(shape)

    xi = lax.broadcasted_iota(jnp.int32, shape, 0)
    yi = lax.broadcasted_iota(jnp.int32, shape, 1)
    parity0 = (xi + yi) & 1
    parity1 = ((xi >> 1) + (yi >> 1)) & 1
    x_low, y_low = (xi & 1) == 0, (yi & 1) == 0
    x_low2, y_low2 = (xi & 2) == 0, (yi & 2) == 0
    edge_x = jnp.logical_or(
        jnp.logical_and(xi == xl, strip == 0), jnp.logical_and(xi == 2 * xl, strip == strips - 1)
    )
    edge_y = yi == 0

    def edge_z(z, width):
        return jnp.logical_or(
            jnp.logical_and(z == width, slab == 0),
            jnp.logical_and(z == 2 * width, slab == slabs - 1),
        )

    table = table_ref[...]
    for block in range(9):
        z_at, x_at = place(block // 3, slab), place(block % 3, strip)

        def soil_step(i, carry, block=block, z_at=z_at, x_at=x_at):
            z = z_at * zl + i
            soil = state_refs[block][zl + i].astype(jnp.int32)
            p = head_refs[block][i]
            forcing = state_refs[block % 3][2 * zl]
            dtheta, alpha, shape_n, k_sat, expon_m = (look_up(table, k, soil) for k in range(5))
            layer = (slab * zl - zl + z).astype(jnp.float32)
            depth = jnp.full((1, ny), layer, jnp.float32)
            sink = forcing * jnp.exp(-ROOT_DECAY * depth / (slabs * zl))
            log_s = jnp.log(jnp.abs(alpha * p))
            log_p = shape_n * log_s
            log_b = jnp.log(1.0 + jnp.exp(log_p))
            root = jnp.exp(-0.5 * expon_m * log_b)
            sat = root * root
            slope = expon_m * shape_n * alpha * sat * jnp.exp((shape_n - 1.0) * log_s - log_b)
            cond[z, x_at] = k_sat * root * jnp.square(1.0 - jnp.exp(expon_m * (log_p - log_b)))
            stor[z, x_at] = slope * (dtheta / DT + sink)
            g = sink * sat
            if first:
                sat_out[z, x_at] = sat
            else:
                g = g + dtheta * (sat - sat_old_ref[z, x_at]) / DT
            grow[z, x_at] = g
            head[z, x_at] = p
            return carry

        lax.fori_loop(0, zl, soil_step, 0)

    def face_z(z):
        both = 0.5 * (slab_of(cond, jnp.maximum(z - 1, 0)) + slab_of(cond, jnp.minimum(z, zw - 1)))
        closed = jnp.logical_or(edge_z(z, zl), jnp.logical_or(z == 0, z == zw))
        return both * jnp.where(closed, 0.0, 1.0)

    fz[0] = jnp.zeros(shape, jnp.float32)

    def face_step(z, carry):
        c, p = slab_of(cond, z), slab_of(head, z)
        across = jnp.where(edge_x, 0.0, 0.5 * (c + roll(c, 1, 0)))
        along = jnp.where(edge_y, 0.0, 0.5 * (c + roll(c, 1, 1)))
        low, high = fz[z], face_z(z + 1)
        flux_x = across * (roll(p, 1, 0) - p)
        flux_y = along * (roll(p, 1, 1) - p)
        p_low = slab_of(head, jnp.maximum(z - 1, 0))
        p_high = slab_of(head, jnp.minimum(z + 1, zw - 1))
        flux_low = low * (p_low - p + GRAVITY)
        flux_high = high * (p - p_high + GRAVITY)
        source = (flux_x - roll(flux_x, -1, 0)) + (flux_y - roll(flux_y, -1, 1))
        source = source + (flux_low - flux_high) - slab_of(grow, z)
        diagonal = slab_of(stor, z) + (across + roll(across, -1, 0)) + (along + roll(along, -1, 1))
        inverse = 1.0 / (diagonal + (low + high))
        fx[z], fy[z], fz[z + 1] = across, along, high
        src[z], inv[z] = source, inverse
        err[z] = jnp.where(parity0 == (z & 1), source * inverse, 0.0)
        return carry

    lax.fori_loop(0, zw, face_step, 0)

    def sum0(z):
        return neighbour_sum(
            err[z],
            err[jnp.maximum(z - 1, 0)],
            err[jnp.minimum(z + 1, zw - 1)],
            fx[z],
            fy[z],
            fz[z],
            fz[z + 1],
            1,
        )

    def smooth_step(z, carry):
        updated = (src[z] + sum0(z)) * inv[z]
        err[z] = jnp.where(parity0 == (z & 1), err[z], updated)
        return carry

    lax.fori_loop(1, zw - 1, smooth_step, 0)

    def coarse_step(k, carry):
        za, zb = 2 * k, 2 * k + 1
        resid = jnp.where(parity0 == 0, sum0(za), sum0(zb))
        src1[k] = spread_pairs(spread_pairs(resid, x_low, 1, 0), y_low, 1, 1)
        stor1[k] = spread_pairs(
            spread_pairs(slab_of(stor, za) + slab_of(stor, zb), x_low, 1, 0), y_low, 1, 1
        )
        across = spread_pairs(fx[za] + fx[zb], y_low, 1, 1)
        fx1[k] = jnp.where(x_low, across, roll(across, 1, 0))
        along = spread_pairs(fy[za] + fy[zb], x_low, 1, 0)
        fy1[k] = jnp.where(y_low, along, roll(along, 1, 1))
        fz1[k] = spread_pairs(spread_pairs(fz[za], x_low, 1, 0), y_low, 1, 1)
        return carry

    lax.fori_loop(1, zw // 2 - 1, coarse_step, 0)

    def first1(k, carry):
        across, along = fx1[k], fy1[k]
        diagonal = stor1[k] + (across + roll(across, -2, 0)) + (along + roll(along, -2, 1))
        inverse = 1.0 / (diagonal + (fz1[k] + fz1[k + 1]))
        inv1[k] = inverse
        err1[k] = jnp.where(parity1 == (k & 1), src1[k] * inverse, 0.0)
        return carry

    low1, high1 = zl // 2 - 2, zl + 2
    lax.fori_loop(low1, high1, first1, 0)

    def sum1(k):
        return neighbour_sum(
            err1[k], err1[k - 1], err1[k + 1], fx1[k], fy1[k], fz1[k], fz1[k + 1], 2
        )

    def second1(k, carry):
        updated = (src1[k] + sum1(k)) * inv1[k]
        err1[k] = jnp.where(parity1 == (k & 1), err1[k], updated)
        return carry

    lax.fori_loop(low1 + 1, high1 - 1, second1, 0)

    rows2[...] = jnp.zeros(rows2.shape, jnp.float32)
    own1 = zl // 2
    for k2 in range(zl // 4):
        ka, kb = own1 + 2 * k2, own1 + 2 * k2 + 1
        resid = jnp.where(parity1 == 0, sum1(ka), sum1(kb))
        terms = (
            spread_pairs(spread_pairs(resid, x_low2, 2, 0), y_low2, 2, 1),
            spread_pairs(spread_pairs(stor1[ka] + stor1[kb], x_low2, 2, 0), y_low2, 2, 1),
            spread_pairs(fx1[ka] + fx1[kb], y_low2, 2, 1),
            spread_pairs(fy1[ka] + fy1[kb], x_low2, 2, 0),
            spread_pairs(spread_pairs(fz1[ka], x_low2, 2, 0), y_low2, 2, 1),
        )
        for t, term in enumerate(terms):
            for x2 in range(xl // 4):
                at = (t * (xl // 4) + x2) * (zl // 4) + k2
                x = xl + 4 * x2
                rows2[at : at + 1, :] = term[x : x + 1, :]
    pick_shape = (ny, ny // 4)
    pick = lax.broadcasted_iota(jnp.int32, pick_shape, 0) == 4 * lax.broadcasted_iota(
        jnp.int32, pick_shape, 1
    )
    payload_ref[0 : rows2.shape[0], :] = jnp.dot(
        rows2[...], jnp.where(pick, 1.0, 0.0), precision=HI, preferred_element_type=jnp.float32
    )
    own = slice(xl, 2 * xl)
    here = [err1[own1 + k][own] for k in range(4)]
    xo, yo = x_low[own], y_low[own]
    plane = jnp.where(xo, jnp.where(yo, here[0], here[1]), jnp.where(yo, here[2], here[3]))
    base = rows2.shape[0]
    for c in range(ny // 128):
        payload_ref[base + 8 * c : base + 8 * c + 8, :] = plane[:, 128 * c : 128 * c + 128]

    def keep0(i, carry):
        for out, ref in zip(outs0, (err, src, inv, fx, fy, fz)):
            out[i] = ref[zl - 2 + i]
        return carry

    lax.fori_loop(0, zl + 4, keep0, 0)

    def keep1(i, carry):
        for out, ref in zip(outs1, (src1, inv1, fx1, fy1, fz1)):
            out[i] = ref[zl // 2 - 2 + i]
        return carry

    lax.fori_loop(0, zl // 2 + 5, keep1, 0)


def solve_blocks(rhs, store, across, vertical, scratch, answer):
    count = rhs.shape[0]
    sub = lax.broadcasted_iota(jnp.int32, (8, 128), 0)
    lane = lax.broadcasted_iota(jnp.int32, (8, 128), 1)
    real = (sub & 1) == 0
    same = lane == sub

    def forward(b, before):
        here_x = jnp.where(real, across[b], 0.0)
        next_x = jnp.where(real, across[b + 1], 0.0)
        low = jnp.where(real, vertical[b], 0.0)
        high = roll(low, -2, 0)
        diagonal = jnp.where(real, store[b] + here_x + next_x + low + high, 1.0)
        m = jnp.where(same, diagonal, 0.0)
        m = m - jnp.where(lane == sub - 2, low, 0.0) - jnp.where(lane == sub + 2, high, 0.0)
        m = m - jnp.where(lane == sub + 8, next_x, 0.0)
        m = m + jnp.where(jnp.logical_and(lane == 16, real), rhs[b], 0.0)
        carried = jnp.where(lane < 8, roll(before, -8, 1), jnp.where(lane == 16, before, 0.0))
        m = m + here_x * carried
        for z in range(0, 8, 2):
            row = m[z : z + 1, :]
            row = row / row[:, z : z + 1]
            m = jnp.where(sub == z, row, m - m[:, z : z + 1] * row)
        scratch[b] = m
        return m

    lax.fori_loop(0, count, forward, jnp.zeros((8, 128), jnp.float32))

    def backward(i, above):
        b = count - 1 - i
        m = scratch[b]
        row = jnp.sum(jnp.where(lane == sub + 8, above, 0.0), axis=0, keepdims=True)
        mask = jnp.logical_and(lane >= 8, lane < 16)
        taken = jnp.where(lane == 16, m, 0.0) - jnp.where(mask, m * row, 0.0)
        value = jnp.broadcast_to(jnp.sum(taken, axis=1, keepdims=True), (8, 128))
        answer[b] = jnp.where(real, value, roll(value, 1, 0))
        return value

    lax.fori_loop(0, count, backward, jnp.zeros((8, 128), jnp.float32))


def up_kernel(slabs, strips, zl, xl, counts, *refs):
    where_ref, refs = refs[0], refs[1:]
    pieces, refs = refs[: len(counts)], refs[len(counts) :]
    near, refs = refs[:3], refs[3:]
    e0_in, src0, inv0, fx0, fy0, fz0 = refs[:6]
    src1, inv1, fx1, fy1, fz1 = refs[6:11]
    head_ref, out_ref = refs[11], refs[12]
    a2, block, answer, e2, picked, wide, e1, e0 = refs[13:]
    strip, slab = where_ref[0], where_ref[1]
    x2, z2 = xl // 4, zl // 4
    rows2 = strips * x2
    ny = head_ref.shape[2]

    index = 0
    for ref, count in zip(pieces, counts):
        for j in range(count):
            at = jnp.bitwise_xor(strip, index)
            for g in range(slabs):
                piece = ref[j, jnp.bitwise_xor(slab, g)]
                for t in range(5):
                    for x in range(x2):
                        k = (t * x2 + x) * z2
                        a2[t, at * x2 + x, g * z2 : g * z2 + z2, :] = piece[k : k + z2, :]
            index += 1

    shape = (rows2, 8, 128)
    source, store, fx, fy, fz = (a2[t] for t in range(5))

    def shift_x(v, step):
        if step > 0:
            return jnp.concatenate([jnp.zeros_like(v[:1]), v[:-1]], axis=0)
        return jnp.concatenate([v[1:], jnp.zeros_like(v[:1])], axis=0)

    def along(v, step, axis):
        return pltpu.roll(v, step % v.shape[axis], axis)

    fx_up, fy_up, fz_up = shift_x(fx, -1), along(fy, -1, 2), along(fz, -1, 1)
    inverse = 1.0 / (store + (fx + fx_up) + (fy + fy_up) + (fz + fz_up))
    parity = (
        lax.broadcasted_iota(jnp.int32, shape, 0)
        + lax.broadcasted_iota(jnp.int32, shape, 1)
        + lax.broadcasted_iota(jnp.int32, shape, 2)
    ) & 1
    even = parity == 0

    def sum2(e):
        total = fx * shift_x(e, 1) + fx_up * shift_x(e, -1)
        total = total + (fy * along(e, 1, 2) + fy_up * along(e, -1, 2))
        return total + (fz * along(e, 1, 1) + fz_up * along(e, -1, 1))

    e = jnp.where(even, source * inverse, 0.0)
    e = jnp.where(even, e, (source + sum2(e)) * inverse)
    resid = jnp.where(even, sum2(e), 0.0)

    def blocks(v, both_rows, both_layers):
        v = v.reshape(strips, x2, 8, 128)
        v = v[:, 0] + v[:, 1] if both_rows else v[:, 0]
        v = jnp.sum(v, axis=2, keepdims=True)
        v = jnp.broadcast_to(v, (strips, 8, 128))
        return v + along(v, -1, 1) if both_layers else v

    block[0, 0:strips] = blocks(resid, True, True)
    block[1, 0:strips] = blocks(store, True, True)
    block[2, 0:strips] = blocks(fx, False, True)
    block[2, strips] = jnp.zeros((8, 128), jnp.float32)
    block[3, 0:strips] = blocks(fz, True, False)
    solve_blocks(
        block.at[0, 0:strips], block.at[1], block.at[2], block.at[3], block.at[4], answer
    )
    add = jnp.broadcast_to(answer[...][:, None], (strips, x2, 8, 128)).reshape(shape)
    e = e + add
    e = jnp.where(even, (source + sum2(e)) * inverse, e)
    e = jnp.where(even, e, (source + sum2(e)) * inverse)
    e2[...] = jnp.zeros(e2.shape, jnp.float32)
    e2[x2 : x2 + rows2, 8:16, :] = e

    picked[...] = jnp.zeros(picked.shape, jnp.float32)
    for z in range(3 * z2):
        for x in range(3 * x2):
            at = z * 3 * x2 + x
            picked[at : at + 1, :] = e2[
                strip * x2 + x, pl.ds(8 - z2 + slab * z2 + z, 1), :
            ]
    spread_shape = (ny // 4, ny)
    spread = lax.broadcasted_iota(jnp.int32, spread_shape, 0) == (
        lax.broadcasted_iota(jnp.int32, spread_shape, 1) >> 2
    )
    wide[...] = jnp.dot(
        picked[...], jnp.where(spread, 1.0, 0.0), precision=HI, preferred_element_type=jnp.float32
    )

    zl1 = zl // 2
    small = (xl, ny)
    xo = (lax.broadcasted_iota(jnp.int32, small, 0) & 1) == 0
    yo = (lax.broadcasted_iota(jnp.int32, small, 1) & 1) == 0
    for zb in range(3):
        g = slab + (zb - 1)
        inside = jnp.logical_and(g >= 0, g < slabs)
        m = jnp.bitwise_xor(slab, jnp.clip(g, 0, slabs - 1))
        keep = jnp.where(inside, 1.0, 0.0)
        for which in range(3):
            xb = place(which, strip)
            tile = near[which][m]
            plane = jnp.concatenate(
                [tile[8 * c : 8 * c + 8, :] for c in range(ny // 128)], axis=1
            )
            plane = plane * keep
            for k in range(4):
                xk, yk = k // 2, k % 2
                v = jnp.where(jnp.logical_and(xo == (xk == 0), yo == (yk == 0)), plane, 0.0)
                v = v + roll(v, 1 if xk == 0 else -1, 0)
                v = v + roll(v, 1 if yk == 0 else -1, 1)
                e1[zb * zl1 + k, xb] = v
    window = (3 * xl, ny)
    for k in range(3 * zl1):
        rows = [wide[k // 2 * 3 * x2 + x : k // 2 * 3 * x2 + x + 1, :] for x in range(3 * x2)]
        rows = [jnp.broadcast_to(row, (4, ny)) for row in rows]
        rows = [jnp.concatenate(rows[x2 * b : x2 * b + x2], axis=0)[None] for b in range(3)]
        e1[k] = e1[k] + jnp.concatenate(rows, axis=0)

    def at1(k):
        return e1[k].reshape(window)

    xi = lax.broadcasted_iota(jnp.int32, window, 0)
    yi = lax.broadcasted_iota(jnp.int32, window, 1)
    parity0 = (xi + yi) & 1
    parity1 = ((xi >> 1) + (yi >> 1)) & 1

    def level1(k, colour):
        i = k - (zl1 - 2)
        total = neighbour_sum(
            at1(k), at1(k - 1), at1(k + 1), fx1[i], fy1[i], fz1[i], fz1[i + 1], 2
        )
        updated = (src1[i] + total) * inv1[i]
        e1[k] = jnp.where(parity1 == ((k + colour) & 1), updated, at1(k)).reshape(3, xl, ny)

    def up1(colour, reach):
        def step(k, carry):
            level1(k, colour)
            return carry

        lax.fori_loop(zl1 - reach, 2 * zl1 + reach, step, 0)

    up1(0, 2)
    up1(1, 1)

    def join(i, carry):
        e0[i] = e0_in[i] + at1((zl - 2 + i) // 2)
        return carry

    lax.fori_loop(0, zl + 4, join, 0)

    def up0(colour, reach):
        def step(i, carry):
            total = neighbour_sum(
                e0[i], e0[i - 1], e0[i + 1], fx0[i], fy0[i], fz0[i], fz0[i + 1], 1
            )
            updated = (src0[i] + total) * inv0[i]
            e0[i] = jnp.where(parity0 == ((i + colour) & 1), updated, e0[i])
            return carry

        lax.fori_loop(2 - reach, zl + 2 + reach, step, 0)

    up0(0, 1)
    up0(1, 0)
    for z in range(zl):
        out_ref[z] = head_ref[z] + e0[z + 2][xl : 2 * xl]


VMEM = pl.BlockSpec(memory_space=pltpu.VMEM)
SMEM = pl.BlockSpec(memory_space=pltpu.SMEM)


def f32(*shape):
    return jax.ShapeDtypeStruct(shape, jnp.float32)


def down(first, slabs, strips, zl, xl, ny, where, table, state, head=None, sat_old=None):
    zw, xw = 3 * zl, 3 * xl
    rows2 = 5 * (xl // 4) * (zl // 4)
    rows2 = -(-rows2 // 8) * 8
    out_shape = [f32(rows2 + 8 * ny // 128, 128)]
    out_shape += [f32(zl + 4, xw, ny)] * 6 + [f32(zl // 2 + 5, xw, ny)] * 5
    operands = [where, table, *state]
    if first:
        out_shape.append(f32(zw, 3, xl, ny))
    else:
        operands += [*head, sat_old]
    split = pltpu.VMEM((zw, 3, xl, ny), jnp.float32)
    full, half = pltpu.VMEM((zw, xw, ny), jnp.float32), pltpu.VMEM((zw // 2, xw, ny), jnp.float32)
    tall = pltpu.VMEM((zw + 1, xw, ny), jnp.float32)
    return pl.pallas_call(
        functools.partial(down_kernel, first, slabs, strips, zl, xl),
        out_shape=out_shape,
        in_specs=[SMEM] + [VMEM] * (len(operands) - 1),
        out_specs=[VMEM] * len(out_shape),
        scratch_shapes=[split] * 4 + [full] * 2 + [tall] + [full] * 3 + [half] * 7
        + [pltpu.VMEM((rows2, ny), jnp.float32)],
        compiler_params=pltpu.CompilerParams(vmem_limit_bytes=44 * 1024 * 1024),
    )(*operands)


def up(slabs, strips, zl, xl, ny, where, pieces, near, kept, head):
    x2, z2 = xl // 4, zl // 4
    counts = [p.shape[0] for p in pieces]
    operands = [where, *pieces, *near, *kept, head]
    n = -(-9 * x2 * z2 // 8) * 8
    scratch = [
        pltpu.VMEM((5, strips * x2, 8, 128), jnp.float32),
        pltpu.VMEM((5, strips + 1, 8, 128), jnp.float32),
        pltpu.VMEM((strips, 8, 128), jnp.float32),
        pltpu.VMEM(((strips + 2) * x2, 24, 128), jnp.float32),
        pltpu.VMEM((n, ny // 4), jnp.float32),
        pltpu.VMEM((n, ny), jnp.float32),
        pltpu.VMEM((3 * zl // 2, 3, xl, ny), jnp.float32),
        pltpu.VMEM((zl + 4, 3 * xl, ny), jnp.float32),
    ]
    return pl.pallas_call(
        functools.partial(up_kernel, slabs, strips, zl, xl, counts),
        out_shape=f32(zl, xl, ny),
        in_specs=[SMEM] + [VMEM] * (len(operands) - 1),
        out_specs=VMEM,
        scratch_shapes=scratch,
        compiler_params=pltpu.CompilerParams(vmem_limit_bytes=44 * 1024 * 1024),
    )(*operands)


def swapped(x, axis, mask):
    return lax.ppermute(x, axis, [(i, i ^ mask) for i in range(lax.axis_size(axis))])


def odd_pairs(x, axis):
    size = lax.axis_size(axis)
    pairs = [(i, i + 1) for i in range(1, size - 1, 2)]
    return lax.ppermute(x, axis, pairs + [(j, i) for i, j in pairs])


def neighbourhood(x):
    row = [x, swapped(x, "xy", 1), odd_pairs(x, "xy")]
    return row + [swapped(v, "gz", 1) for v in row] + [odd_pairs(v, "gz") for v in row]


def gather_strips(own, partner):
    size = lax.axis_size("xy")
    x = jnp.stack([own, partner])
    if size == 8:
        return [x] + [swapped(x, "xy", m) for m in (2, 4, 6)]
    mask = 2
    while mask < size:
        x = jnp.concatenate([x, swapped(x, "xy", mask)])
        mask *= 2
    return [x]


def per_device(head_old, soil_type, soil_table, land_mask, sun_bin):
    zl, xl, ny = head_old.shape
    strips, slabs = lax.axis_size("xy"), lax.axis_size("gz")
    where = jnp.stack([lax.axis_index("xy"), lax.axis_index("gz")]).astype(jnp.int32)
    resid, sat, alpha, shape_n, k_sat = soil_table
    table = jnp.stack([sat - resid, alpha, shape_n, k_sat, 1.0 - 1.0 / shape_n])
    table = jnp.pad(table, ((0, 3), (0, 128 - table.shape[1])))
    sun_share = jnp.maximum(0.0, jnp.sin(math.pi * (sun_bin.astype(jnp.float32) - 6.0) / 12.0))
    forcing = ET_PEAK * sun_share * land_mask.astype(jnp.float32)
    own = jnp.concatenate([head_old, soil_type.astype(jnp.float32), forcing[None]])
    state = neighbourhood(own)
    sizes = (slabs, strips, zl, xl, ny)
    base = -(-5 * (xl // 4) * (zl // 4) // 8) * 8

    def finish(payload, kept, head):
        slab = [payload] + [swapped(payload, "gz", m) for m in range(1, slabs)]
        full = jnp.stack(slab)
        partner = swapped(full, "xy", 1)
        pieces = gather_strips(full[:, :base], partner[:, :base])
        near = [full[:, base:], partner[:, base:], odd_pairs(full[:, base:], "xy")]
        return up(*sizes, where, pieces, near, kept, head)

    payload, *kept, sat_old = down(True, *sizes, where, table, state)
    head = finish(payload, kept, head_old)
    payload, *kept = down(False, *sizes, where, table, state, neighbourhood(head), sat_old)
    return finish(payload, kept, head)


def solution(mesh):
    in_specs = (P("gz", "xy", None), P("gz", "xy", None), P(), P("xy", None), P("xy", None))
    out_specs = P("gz", "xy", None)
    return jax.shard_map(
        per_device, mesh=mesh, in_specs=in_specs, out_specs=out_specs, check_vma=False
    )
```

```python
import functools
import math

import jax
import jax.numpy as jnp
from jax import lax
from jax.experimental import pallas as pl
from jax.experimental.pallas import tpu as pltpu
from jax.sharding import PartitionSpec as P

DT = 20.0
ET_PEAK = 0.008
GRAVITY = 0.1
ROOT_DECAY = 3.0
HI = lax.Precision.HIGHEST


def roll(value, shift, axis):
    return pltpu.roll(value, shift % value.shape[axis], axis)


def place(which, index):
    if which == 0:
        return 1
    odd = index & 1
    return 2 - 2 * odd if which == 1 else 2 * odd


def spread_pairs(value, low, step, axis):
    return value + jnp.where(low, roll(value, -step, axis), roll(value, step, axis))


def neighbour_sum(e, below, above, fx, fy, fz, fz_up, step):
    total = fx * roll(e, step, 0) + roll(fx * e, -step, 0)
    total = total + (fy * roll(e, step, 1) + roll(fy * e, -step, 1))
    return total + (fz * below + fz_up * above)


def look_up(table, row, index):
    picked = jnp.broadcast_to(table[row : row + 1, :], (8, 128))
    rows = []
    for r in range(0, index.shape[0], 8):
        cols = []
        for c in range(0, index.shape[1], 128):
            at = index[r : r + 8, c : c + 128]
            cols.append(jnp.take_along_axis(picked, at, axis=1, mode="promise_in_bounds"))
        rows.append(jnp.concatenate(cols, axis=1))
    return jnp.concatenate(rows, axis=0)


def down_kernel(first, slabs, strips, zl, xl, *refs):
    where_ref, table_ref = refs[0], refs[1]
    refs = refs[2:]
    state_refs, refs = refs[:9], refs[9:]
    if first:
        head_refs = state_refs
    else:
        head_refs, refs = refs[:9], refs[9:]
        sat_old_ref, refs = refs[0], refs[1:]
    payload_ref, refs = refs[0], refs[1:]
    outs0, refs = refs[:6], refs[6:]
    outs1, refs = refs[:5], refs[5:]
    if first:
        sat_out, refs = refs[0], refs[1:]
    head, cond, stor, grow, fx, fy, fz, src, inv, err = refs[:10]
    src1, stor1, fx1, fy1, fz1, inv1, err1, rows2, table_rows = refs[10:]

    strip, slab = where_ref[0], where_ref[1]
    zw, xw = 3 * zl, 3 * xl
    ny = head.shape[3]
    shape = (xw, ny)

    def slab_of(ref, z):
        return ref[z].reshape(shape)

    xi = lax.broadcasted_iota(jnp.int32, shape, 0)
    yi = lax.broadcasted_iota(jnp.int32, shape, 1)
    parity0 = (xi + yi) & 1
    parity1 = ((xi >> 1) + (yi >> 1)) & 1
    x_low, y_low = (xi & 1) == 0, (yi & 1) == 0
    x_low2, y_low2 = (xi & 2) == 0, (yi & 2) == 0
    edge_x = jnp.logical_or(
        jnp.logical_and(xi == xl, strip == 0), jnp.logical_and(xi == 2 * xl, strip == strips - 1)
    )
    edge_y = yi == 0

    def edge_z(z, width):
        return jnp.logical_or(
            jnp.logical_and(z == width, slab == 0),
            jnp.logical_and(z == 2 * width, slab == slabs - 1),
        )

    resid, high, alpha, shape_n, k_sat = (table_ref[k : k + 1, :] for k in range(5))
    classes = table_ref.shape[1]
    rows = (high - resid, alpha, shape_n, k_sat, 1.0 - 1.0 / shape_n)
    table_rows[...] = jnp.ones(table_rows.shape, jnp.float32)
    for k, row in enumerate(rows):
        table_rows[k : k + 1, 0:classes] = row
    table = table_rows[...]
    for block in range(9):
        z_at, x_at = place(block // 3, slab), place(block % 3, strip)

        def soil_step(i, carry, block=block, z_at=z_at, x_at=x_at):
            z = z_at * zl + i
            soil = state_refs[block][zl + i].astype(jnp.int32)
            p = head_refs[block][i]
            forcing = state_refs[block % 3][2 * zl]
            dtheta, alpha, shape_n, k_sat, expon_m = (look_up(table, k, soil) for k in range(5))
            layer = (slab * zl - zl + z).astype(jnp.float32)
            depth = jnp.full((1, ny), layer, jnp.float32)
            sink = forcing * jnp.exp(-ROOT_DECAY * depth / (slabs * zl))
            log_s = jnp.log(jnp.abs(alpha * p))
            log_p = shape_n * log_s
            log_b = jnp.log(1.0 + jnp.exp(log_p))
            root = jnp.exp(-0.5 * expon_m * log_b)
            sat = root * root
            slope = expon_m * shape_n * alpha * sat * jnp.exp((shape_n - 1.0) * log_s - log_b)
            cond[z, x_at] = k_sat * root * jnp.square(1.0 - jnp.exp(expon_m * (log_p - log_b)))
            stor[z, x_at] = slope * (dtheta / DT + sink)
            g = sink * sat
            if first:
                sat_out[z, x_at] = sat
            else:
                g = g + dtheta * (sat - sat_old_ref[z, x_at]) / DT
            grow[z, x_at] = g
            head[z, x_at] = p
            return carry

        skip = 0 if block < 3 else 1
        start = jnp.where(z_at == 0, skip, 0)
        lax.fori_loop(0, zl - skip, lambda i, c: soil_step(start + i, c), 0, unroll=zl - skip)

    def face_z(z):
        both = 0.5 * (slab_of(cond, z - 1) + slab_of(cond, z))
        return both * jnp.where(edge_z(z, zl), 0.0, 1.0)

    fz[2] = face_z(2)

    def face_step(z, carry):
        c, p = slab_of(cond, z), slab_of(head, z)
        across = jnp.where(edge_x, 0.0, 0.5 * (c + roll(c, 1, 0)))
        along = jnp.where(edge_y, 0.0, 0.5 * (c + roll(c, 1, 1)))
        low, high = fz[z], face_z(z + 1)
        flux_x = across * (roll(p, 1, 0) - p)
        flux_y = along * (roll(p, 1, 1) - p)
        p_low = slab_of(head, z - 1)
        p_high = slab_of(head, z + 1)
        flux_low = low * (p_low - p + GRAVITY)
        flux_high = high * (p - p_high + GRAVITY)
        source = (flux_x - roll(flux_x, -1, 0)) + (flux_y - roll(flux_y, -1, 1))
        source = source + (flux_low - flux_high) - slab_of(grow, z)
        diagonal = slab_of(stor, z) + (across + roll(across, -1, 0)) + (along + roll(along, -1, 1))
        inverse = 1.0 / (diagonal + (low + high))
        fx[z], fy[z], fz[z + 1] = across, along, high
        src[z], inv[z] = source, inverse
        err[z] = jnp.where(parity0 == (z & 1), source * inverse, 0.0)
        return carry

    lax.fori_loop(2, zw - 2, face_step, 0, unroll=4)

    def sum0(z):
        return neighbour_sum(
            err[z],
            err[z - 1],
            err[z + 1],
            fx[z],
            fy[z],
            fz[z],
            fz[z + 1],
            1,
        )

    def smooth_step(z, carry):
        updated = (src[z] + sum0(z)) * inv[z]
        err[z] = jnp.where(parity0 == (z & 1), err[z], updated)
        return carry

    lax.fori_loop(3, zw - 3, smooth_step, 0, unroll=3)

    def coarse_step(k, carry):
        za, zb = 2 * k, 2 * k + 1
        resid = jnp.where(parity0 == 0, sum0(za), sum0(zb))
        src1[k] = spread_pairs(spread_pairs(resid, x_low, 1, 0), y_low, 1, 1)
        stor1[k] = spread_pairs(
            spread_pairs(slab_of(stor, za) + slab_of(stor, zb), x_low, 1, 0), y_low, 1, 1
        )
        across = spread_pairs(fx[za] + fx[zb], y_low, 1, 1)
        fx1[k] = jnp.where(x_low, across, roll(across, 1, 0))
        along = spread_pairs(fy[za] + fy[zb], x_low, 1, 0)
        fy1[k] = jnp.where(y_low, along, roll(along, 1, 1))
        fz1[k] = spread_pairs(spread_pairs(fz[za], x_low, 1, 0), y_low, 1, 1)
        return carry

    lax.fori_loop(2, zw // 2 - 1, coarse_step, 0, unroll=3)

    def first1(k, carry):
        across, along = fx1[k], fy1[k]
        diagonal = stor1[k] + (across + roll(across, -2, 0)) + (along + roll(along, -2, 1))
        inverse = 1.0 / (diagonal + (fz1[k] + fz1[k + 1]))
        inv1[k] = inverse
        err1[k] = jnp.where(parity1 == (k & 1), src1[k] * inverse, 0.0)
        return carry

    low1, high1 = zl // 2 - 2, zl + 2
    lax.fori_loop(low1, high1, first1, 0, unroll=4)

    def sum1(k):
        return neighbour_sum(
            err1[k], err1[k - 1], err1[k + 1], fx1[k], fy1[k], fz1[k], fz1[k + 1], 2
        )

    def second1(k, carry):
        updated = (src1[k] + sum1(k)) * inv1[k]
        err1[k] = jnp.where(parity1 == (k & 1), err1[k], updated)
        return carry

    lax.fori_loop(low1 + 1, high1 - 1, second1, 0, unroll=3)

    rows2[...] = jnp.zeros(rows2.shape, jnp.float32)
    own1 = zl // 2
    for k2 in range(zl // 4):
        ka, kb = own1 + 2 * k2, own1 + 2 * k2 + 1
        resid = jnp.where(parity1 == 0, sum1(ka), sum1(kb))
        terms = (
            spread_pairs(spread_pairs(resid, x_low2, 2, 0), y_low2, 2, 1),
            spread_pairs(spread_pairs(stor1[ka] + stor1[kb], x_low2, 2, 0), y_low2, 2, 1),
            spread_pairs(fx1[ka] + fx1[kb], y_low2, 2, 1),
            spread_pairs(fy1[ka] + fy1[kb], x_low2, 2, 0),
            spread_pairs(spread_pairs(fz1[ka], x_low2, 2, 0), y_low2, 2, 1),
        )
        for t, term in enumerate(terms):
            for x2 in range(xl // 4):
                at = (t * (xl // 4) + x2) * (zl // 4) + k2
                x = xl + 4 * x2
                rows2[at : at + 1, :] = term[x : x + 1, :]
    pick_shape = (ny, ny // 4)
    pick = lax.broadcasted_iota(jnp.int32, pick_shape, 0) == 4 * lax.broadcasted_iota(
        jnp.int32, pick_shape, 1
    )
    payload_ref[0 : rows2.shape[0], :] = jnp.dot(
        rows2[...], jnp.where(pick, 1.0, 0.0), precision=HI, preferred_element_type=jnp.float32
    )
    own = slice(xl, 2 * xl)
    here = [err1[own1 + k][own] for k in range(4)]
    xo, yo = x_low[own], y_low[own]
    plane = jnp.where(xo, jnp.where(yo, here[0], here[1]), jnp.where(yo, here[2], here[3]))
    base = rows2.shape[0]
    for c in range(ny // 128):
        payload_ref[base + 8 * c : base + 8 * c + 8, :] = plane[:, 128 * c : 128 * c + 128]

    def keep0(i, carry):
        for out, ref in zip(outs0, (err, src, inv, fx, fy, fz)):
            out[i] = ref[zl - 2 + i]
        return carry

    lax.fori_loop(0, zl + 4, keep0, 0, unroll=3)

    def keep1(i, carry):
        for out, ref in zip(outs1, (src1, inv1, fx1, fy1, fz1)):
            out[i] = ref[zl // 2 - 2 + i]
        return carry

    lax.fori_loop(0, zl // 2 + 5, keep1, 0, unroll=3)


def solve_blocks(rhs, store, across, vertical, scratch, answer):
    count = rhs.shape[0]
    sub = lax.broadcasted_iota(jnp.int32, (8, 128), 0)
    lane = lax.broadcasted_iota(jnp.int32, (8, 128), 1)
    real = (sub & 1) == 0
    same = lane == sub

    def forward(b, before):
        here_x = jnp.where(real, across[b], 0.0)
        next_x = jnp.where(real, across[b + 1], 0.0)
        low = jnp.where(real, vertical[b], 0.0)
        high = roll(low, -2, 0)
        diagonal = jnp.where(real, store[b] + here_x + next_x + low + high, 1.0)
        m = jnp.where(same, diagonal, 0.0)
        m = m - jnp.where(lane == sub - 2, low, 0.0) - jnp.where(lane == sub + 2, high, 0.0)
        m = m - jnp.where(lane == sub + 8, next_x, 0.0)
        m = m + jnp.where(jnp.logical_and(lane == 16, real), rhs[b], 0.0)
        carried = jnp.where(lane < 8, roll(before, -8, 1), jnp.where(lane == 16, before, 0.0))
        m = m + here_x * carried
        for z in range(0, 8, 2):
            row = m[z : z + 1, :]
            row = row / row[:, z : z + 1]
            m = jnp.where(sub == z, row, m - m[:, z : z + 1] * row)
        scratch[b] = m
        return m

    lax.fori_loop(0, count, forward, jnp.zeros((8, 128), jnp.float32))

    def backward(i, above):
        b = count - 1 - i
        m = scratch[b]
        row = jnp.sum(jnp.where(lane == sub + 8, above, 0.0), axis=0, keepdims=True)
        mask = jnp.logical_and(lane >= 8, lane < 16)
        taken = jnp.where(lane == 16, m, 0.0) - jnp.where(mask, m * row, 0.0)
        value = jnp.broadcast_to(jnp.sum(taken, axis=1, keepdims=True), (8, 128))
        answer[b] = jnp.where(real, value, roll(value, 1, 0))
        return value

    lax.fori_loop(0, count, backward, jnp.zeros((8, 128), jnp.float32))


def up_kernel(slabs, strips, zl, xl, counts, *refs):
    where_ref, refs = refs[0], refs[1:]
    pieces, refs = refs[: len(counts)], refs[len(counts) :]
    near, refs = refs[:3], refs[3:]
    e0_in, src0, inv0, fx0, fy0, fz0 = refs[:6]
    src1, inv1, fx1, fy1, fz1 = refs[6:11]
    head_ref, out_ref = refs[11], refs[12]
    a2, block, answer, e2, picked, wide, e1, e0 = refs[13:]
    strip, slab = where_ref[0], where_ref[1]
    x2, z2 = xl // 4, zl // 4
    rows2 = strips * x2
    ny = head_ref.shape[2]

    index = 0
    for ref, count in zip(pieces, counts):
        for j in range(count):
            at = jnp.bitwise_xor(strip, index)
            for g in range(slabs):
                piece = ref[j, jnp.bitwise_xor(slab, g)]
                for t in range(5):
                    for x in range(x2):
                        k = (t * x2 + x) * z2
                        a2[t, at * x2 + x, g * z2 : g * z2 + z2, :] = piece[k : k + z2, :]
            index += 1

    shape = (rows2, 8, 128)
    source, store, fx, fy, fz = (a2[t] for t in range(5))

    def shift_x(v, step):
        if step > 0:
            return jnp.concatenate([jnp.zeros_like(v[:1]), v[:-1]], axis=0)
        return jnp.concatenate([v[1:], jnp.zeros_like(v[:1])], axis=0)

    def along(v, step, axis):
        return pltpu.roll(v, step % v.shape[axis], axis)

    fx_up, fy_up, fz_up = shift_x(fx, -1), along(fy, -1, 2), along(fz, -1, 1)
    inverse = 1.0 / (store + (fx + fx_up) + (fy + fy_up) + (fz + fz_up))
    parity = (
        lax.broadcasted_iota(jnp.int32, shape, 0)
        + lax.broadcasted_iota(jnp.int32, shape, 1)
        + lax.broadcasted_iota(jnp.int32, shape, 2)
    ) & 1
    even = parity == 0

    def sum2(e):
        total = fx * shift_x(e, 1) + fx_up * shift_x(e, -1)
        total = total + (fy * along(e, 1, 2) + fy_up * along(e, -1, 2))
        return total + (fz * along(e, 1, 1) + fz_up * along(e, -1, 1))

    e = jnp.where(even, source * inverse, 0.0)
    e = jnp.where(even, e, (source + sum2(e)) * inverse)
    resid = jnp.where(even, sum2(e), 0.0)

    def blocks(v, both_rows, both_layers):
        v = v.reshape(strips, x2, 8, 128)
        v = v[:, 0] + v[:, 1] if both_rows else v[:, 0]
        v = jnp.sum(v, axis=2, keepdims=True)
        v = jnp.broadcast_to(v, (strips, 8, 128))
        return v + along(v, -1, 1) if both_layers else v

    block[0, 0:strips] = blocks(resid, True, True)
    block[1, 0:strips] = blocks(store, True, True)
    block[2, 0:strips] = blocks(fx, False, True)
    block[2, strips] = jnp.zeros((8, 128), jnp.float32)
    block[3, 0:strips] = blocks(fz, True, False)
    solve_blocks(
        block.at[0, 0:strips], block.at[1], block.at[2], block.at[3], block.at[4], answer
    )
    add = jnp.broadcast_to(answer[...][:, None], (strips, x2, 8, 128)).reshape(shape)
    e = e + add
    e = jnp.where(even, (source + sum2(e)) * inverse, e)
    e = jnp.where(even, e, (source + sum2(e)) * inverse)
    e2[...] = jnp.zeros(e2.shape, jnp.float32)
    e2[x2 : x2 + rows2, 8:16, :] = e

    picked[...] = jnp.zeros(picked.shape, jnp.float32)
    for z in range(3 * z2):
        for x in range(3 * x2):
            at = z * 3 * x2 + x
            picked[at : at + 1, :] = e2[
                strip * x2 + x, pl.ds(8 - z2 + slab * z2 + z, 1), :
            ]
    spread_shape = (ny // 4, ny)
    spread = lax.broadcasted_iota(jnp.int32, spread_shape, 0) == (
        lax.broadcasted_iota(jnp.int32, spread_shape, 1) >> 2
    )
    wide[...] = jnp.dot(
        picked[...], jnp.where(spread, 1.0, 0.0), precision=HI, preferred_element_type=jnp.float32
    )

    zl1 = zl // 2
    small = (xl, ny)
    xo = (lax.broadcasted_iota(jnp.int32, small, 0) & 1) == 0
    yo = (lax.broadcasted_iota(jnp.int32, small, 1) & 1) == 0
    for zb in range(3):
        g = slab + (zb - 1)
        inside = jnp.logical_and(g >= 0, g < slabs)
        m = jnp.bitwise_xor(slab, jnp.clip(g, 0, slabs - 1))
        keep = jnp.where(inside, 1.0, 0.0)
        for which in range(3):
            xb = place(which, strip)
            tile = near[which][m]
            plane = jnp.concatenate(
                [tile[8 * c : 8 * c + 8, :] for c in range(ny // 128)], axis=1
            )
            plane = plane * keep
            for k in range(4):
                xk, yk = k // 2, k % 2
                v = jnp.where(jnp.logical_and(xo == (xk == 0), yo == (yk == 0)), plane, 0.0)
                v = v + roll(v, 1 if xk == 0 else -1, 0)
                v = v + roll(v, 1 if yk == 0 else -1, 1)
                e1[zb * zl1 + k, xb] = v
    window = (3 * xl, ny)
    for k in range(3 * zl1):
        rows = [wide[k // 2 * 3 * x2 + x : k // 2 * 3 * x2 + x + 1, :] for x in range(3 * x2)]
        rows = [jnp.broadcast_to(row, (4, ny)) for row in rows]
        rows = [jnp.concatenate(rows[x2 * b : x2 * b + x2], axis=0)[None] for b in range(3)]
        e1[k] = e1[k] + jnp.concatenate(rows, axis=0)

    def at1(k):
        return e1[k].reshape(window)

    xi = lax.broadcasted_iota(jnp.int32, window, 0)
    yi = lax.broadcasted_iota(jnp.int32, window, 1)
    parity0 = (xi + yi) & 1
    parity1 = ((xi >> 1) + (yi >> 1)) & 1

    def level1(k, colour):
        i = k - (zl1 - 2)
        total = neighbour_sum(
            at1(k), at1(k - 1), at1(k + 1), fx1[i], fy1[i], fz1[i], fz1[i + 1], 2
        )
        updated = (src1[i] + total) * inv1[i]
        e1[k] = jnp.where(parity1 == ((k + colour) & 1), updated, at1(k)).reshape(3, xl, ny)

    def up1(colour, reach):
        def step(k, carry):
            level1(k, colour)
            return carry

        lax.fori_loop(zl1 - reach, 2 * zl1 + reach, step, 0, unroll=2)

    up1(0, 2)
    up1(1, 1)

    def join(i, carry):
        e0[i] = e0_in[i] + at1((zl - 2 + i) // 2)
        return carry

    lax.fori_loop(0, zl + 4, join, 0, unroll=3)

    def up0(colour, reach):
        def step(i, carry):
            total = neighbour_sum(
                e0[i], e0[i - 1], e0[i + 1], fx0[i], fy0[i], fz0[i], fz0[i + 1], 1
            )
            updated = (src0[i] + total) * inv0[i]
            e0[i] = jnp.where(parity0 == ((i + colour) & 1), updated, e0[i])
            return carry

        lax.fori_loop(2 - reach, zl + 2 + reach, step, 0, unroll=2)

    up0(0, 1)
    up0(1, 0)
    for z in range(zl):
        out_ref[z] = head_ref[z] + e0[z + 2][xl : 2 * xl]


VMEM = pl.BlockSpec(memory_space=pltpu.VMEM)
SMEM = pl.BlockSpec(memory_space=pltpu.SMEM)


def f32(*shape):
    return jax.ShapeDtypeStruct(shape, jnp.float32)


def down(first, slabs, strips, zl, xl, ny, where, table, state, head=None, sat_old=None):
    zw, xw = 3 * zl, 3 * xl
    rows2 = 5 * (xl // 4) * (zl // 4)
    rows2 = -(-rows2 // 8) * 8
    out_shape = [f32(rows2 + 8 * ny // 128, 128)]
    out_shape += [f32(zl + 4, xw, ny)] * 6 + [f32(zl // 2 + 5, xw, ny)] * 5
    operands = [where, table, *state]
    if first:
        out_shape.append(f32(zw, 3, xl, ny))
    else:
        operands += [*head, sat_old]
    split = pltpu.VMEM((zw, 3, xl, ny), jnp.float32)
    full, half = pltpu.VMEM((zw, xw, ny), jnp.float32), pltpu.VMEM((zw // 2, xw, ny), jnp.float32)
    tall = pltpu.VMEM((zw + 1, xw, ny), jnp.float32)
    return pl.pallas_call(
        functools.partial(down_kernel, first, slabs, strips, zl, xl),
        out_shape=out_shape,
        in_specs=[SMEM] + [VMEM] * (len(operands) - 1),
        out_specs=[VMEM] * len(out_shape),
        scratch_shapes=[split] * 4 + [full] * 2 + [tall] + [full] * 3 + [half] * 7
        + [pltpu.VMEM((rows2, ny), jnp.float32), pltpu.VMEM((8, 128), jnp.float32)],
        compiler_params=pltpu.CompilerParams(vmem_limit_bytes=44 * 1024 * 1024),
    )(*operands)


def up(slabs, strips, zl, xl, ny, where, pieces, near, kept, head):
    x2, z2 = xl // 4, zl // 4
    counts = [p.shape[0] for p in pieces]
    operands = [where, *pieces, *near, *kept, head]
    n = -(-9 * x2 * z2 // 8) * 8
    scratch = [
        pltpu.VMEM((5, strips * x2, 8, 128), jnp.float32),
        pltpu.VMEM((5, strips + 1, 8, 128), jnp.float32),
        pltpu.VMEM((strips, 8, 128), jnp.float32),
        pltpu.VMEM(((strips + 2) * x2, 24, 128), jnp.float32),
        pltpu.VMEM((n, ny // 4), jnp.float32),
        pltpu.VMEM((n, ny), jnp.float32),
        pltpu.VMEM((3 * zl // 2, 3, xl, ny), jnp.float32),
        pltpu.VMEM((zl + 4, 3 * xl, ny), jnp.float32),
    ]
    return pl.pallas_call(
        functools.partial(up_kernel, slabs, strips, zl, xl, counts),
        out_shape=f32(zl, xl, ny),
        in_specs=[SMEM] + [VMEM] * (len(operands) - 1),
        out_specs=VMEM,
        scratch_shapes=scratch,
        compiler_params=pltpu.CompilerParams(vmem_limit_bytes=44 * 1024 * 1024),
    )(*operands)


def swapped(x, axis, mask):
    return lax.ppermute(x, axis, [(i, i ^ mask) for i in range(lax.axis_size(axis))])


def odd_pairs(x, axis):
    size = lax.axis_size(axis)
    pairs = [(i, i + 1) for i in range(1, size - 1, 2)]
    return lax.ppermute(x, axis, pairs + [(j, i) for i, j in pairs])


def neighbourhood(x):
    row = [x, swapped(x, "xy", 1), odd_pairs(x, "xy")]
    return row + [swapped(v, "gz", 1) for v in row] + [odd_pairs(v, "gz") for v in row]


def gather_strips(own, partner):
    size = lax.axis_size("xy")
    x = jnp.stack([own, partner])
    if size == 8:
        return [x] + [swapped(x, "xy", m) for m in (2, 4, 6)]
    mask = 2
    while mask < size:
        x = jnp.concatenate([x, swapped(x, "xy", mask)])
        mask *= 2
    return [x]


def per_device(head_old, soil_type, soil_table, land_mask, sun_bin):
    zl, xl, ny = head_old.shape
    strips, slabs = lax.axis_size("xy"), lax.axis_size("gz")
    where = jnp.stack([lax.axis_index("xy"), lax.axis_index("gz")]).astype(jnp.int32)
    sun_share = jnp.maximum(0.0, jnp.sin(math.pi * (sun_bin.astype(jnp.float32) - 6.0) / 12.0))
    forcing = ET_PEAK * sun_share * land_mask.astype(jnp.float32)
    own = jnp.concatenate([head_old, soil_type.astype(jnp.float32), forcing[None]])
    state = neighbourhood(own)
    sizes = (slabs, strips, zl, xl, ny)
    base = -(-5 * (xl // 4) * (zl // 4) // 8) * 8

    def finish(payload, kept, head):
        slab = [payload] + [swapped(payload, "gz", m) for m in range(1, slabs)]
        full = jnp.stack(slab)
        partner = swapped(full, "xy", 1)
        pieces = gather_strips(full[:, :base], partner[:, :base])
        near = [full[:, base:], partner[:, base:], odd_pairs(full[:, base:], "xy")]
        return up(*sizes, where, pieces, near, kept, head)

    payload, *kept, sat_old = down(True, *sizes, where, soil_table, state)
    head = finish(payload, kept, head_old)
    payload, *kept = down(
        False, *sizes, where, soil_table, state, neighbourhood(head), sat_old
    )
    return finish(payload, kept, head)


def solution(mesh):
    in_specs = (P("gz", "xy", None), P("gz", "xy", None), P(), P("xy", None), P("xy", None))
    out_specs = P("gz", "xy", None)
    return jax.shard_map(
        per_device, mesh=mesh, in_specs=in_specs, out_specs=out_specs, check_vma=False
    )
```

```python
import functools
import math

import jax
import jax.numpy as jnp
from jax import lax
from jax.experimental import pallas as pl
from jax.experimental.pallas import tpu as pltpu
from jax.sharding import PartitionSpec as P

DT = 20.0
ET_PEAK = 0.008
GRAVITY = 0.1
ROOT_DECAY = 3.0
HI = lax.Precision.HIGHEST


def roll(value, shift, axis):
    return pltpu.roll(value, shift % value.shape[axis], axis)


def place(which, index):
    if which == 0:
        return 1
    odd = index & 1
    return 2 - 2 * odd if which == 1 else 2 * odd


def spread_pairs(value, low, step, axis):
    return value + jnp.where(low, roll(value, -step, axis), roll(value, step, axis))


def neighbour_sum(e, below, above, fx, fy, fz, fz_up, step):
    total = fx * roll(e, step, 0) + roll(fx * e, -step, 0)
    total = total + (fy * roll(e, step, 1) + roll(fy * e, -step, 1))
    return total + (fz * below + fz_up * above)


def look_up(table, row, index):
    picked = jnp.broadcast_to(table[row : row + 1, :], (8, 128))
    rows = []
    for r in range(0, index.shape[0], 8):
        cols = []
        for c in range(0, index.shape[1], 128):
            at = index[r : r + 8, c : c + 128]
            cols.append(jnp.take_along_axis(picked, at, axis=1, mode="promise_in_bounds"))
        rows.append(jnp.concatenate(cols, axis=1))
    return jnp.concatenate(rows, axis=0)


def down_kernel(first, slabs, strips, zl, xl, *refs):
    where_ref, table_ref = refs[0], refs[1]
    refs = refs[2:]
    state_refs, refs = refs[:9], refs[9:]
    if first:
        head_refs = state_refs
    else:
        head_refs, refs = refs[:9], refs[9:]
        sat_old_ref, refs = refs[0], refs[1:]
    payload_ref, refs = refs[0], refs[1:]
    outs0, refs = refs[:6], refs[6:]
    outs1, refs = refs[:5], refs[5:]
    if first:
        sat_out, refs = refs[0], refs[1:]
    head, cond, stor, grow, fx, fy, fz, src, inv, err = refs[:10]
    src1, stor1, fx1, fy1, fz1, inv1, err1, rows2, table_rows = refs[10:]

    strip, slab = where_ref[0], where_ref[1]
    zw, xw = 3 * zl, 3 * xl
    ny = head.shape[3]
    shape = (xw, ny)

    def slab_of(ref, z):
        return ref[z].reshape(shape)

    xi = lax.broadcasted_iota(jnp.int32, shape, 0)
    yi = lax.broadcasted_iota(jnp.int32, shape, 1)
    parity0 = (xi + yi) & 1
    parity1 = ((xi >> 1) + (yi >> 1)) & 1
    x_low, y_low = (xi & 1) == 0, (yi & 1) == 0
    x_low2, y_low2 = (xi & 2) == 0, (yi & 2) == 0
    edge_x = jnp.logical_or(
        jnp.logical_and(xi == xl, strip == 0), jnp.logical_and(xi == 2 * xl, strip == strips - 1)
    )
    edge_y = yi == 0

    def edge_z(z, width):
        return jnp.logical_or(
            jnp.logical_and(z == width, slab == 0),
            jnp.logical_and(z == 2 * width, slab == slabs - 1),
        )

    resid, high, alpha, shape_n, k_sat = (table_ref[k : k + 1, :] for k in range(5))
    classes = table_ref.shape[1]
    rows = (high - resid, alpha, shape_n, k_sat, 1.0 - 1.0 / shape_n)
    table_rows[...] = jnp.ones(table_rows.shape, jnp.float32)
    for k, row in enumerate(rows):
        table_rows[k : k + 1, 0:classes] = row
    table = table_rows[...]
    for block in range(9):
        z_at, x_at = place(block // 3, slab), place(block % 3, strip)

        def soil_step(i, carry, block=block, z_at=z_at, x_at=x_at):
            z = z_at * zl + i
            soil = state_refs[block][zl + i].astype(jnp.int32)
            p = head_refs[block][i]
            forcing = state_refs[block % 3][2 * zl]
            dtheta, alpha, shape_n, k_sat, expon_m = (look_up(table, k, soil) for k in range(5))
            layer = (slab * zl - zl + z).astype(jnp.float32)
            depth = jnp.full((1, ny), layer, jnp.float32)
            sink = forcing * jnp.exp(-ROOT_DECAY * depth / (slabs * zl))
            log_s = jnp.log(jnp.abs(alpha * p))
            log_p = shape_n * log_s
            log_b = jnp.log(1.0 + jnp.exp(log_p))
            root = jnp.exp(-0.5 * expon_m * log_b)
            sat = root * root
            slope = expon_m * shape_n * alpha * sat * jnp.exp((shape_n - 1.0) * log_s - log_b)
            cond[z, x_at] = k_sat * root * jnp.square(1.0 - jnp.exp(expon_m * (log_p - log_b)))
            stor[z, x_at] = slope * (dtheta / DT + sink)
            g = sink * sat
            if first:
                sat_out[z, x_at] = sat
            else:
                g = g + dtheta * (sat - sat_old_ref[z, x_at]) / DT
            grow[z, x_at] = g
            head[z, x_at] = p
            return carry

        skip = 0 if block < 3 else 1
        start = jnp.where(z_at == 0, skip, 0)
        lax.fori_loop(0, zl - skip, lambda i, c: soil_step(start + i, c), 0, unroll=zl - skip)

    def face_z(z):
        both = 0.5 * (slab_of(cond, z - 1) + slab_of(cond, z))
        return both * jnp.where(edge_z(z, zl), 0.0, 1.0)

    fz[2] = face_z(2)

    def face_step(z, carry):
        c, p = slab_of(cond, z), slab_of(head, z)
        across = jnp.where(edge_x, 0.0, 0.5 * (c + roll(c, 1, 0)))
        along = jnp.where(edge_y, 0.0, 0.5 * (c + roll(c, 1, 1)))
        low, high = fz[z], face_z(z + 1)
        flux_x = across * (roll(p, 1, 0) - p)
        flux_y = along * (roll(p, 1, 1) - p)
        p_low = slab_of(head, z - 1)
        p_high = slab_of(head, z + 1)
        flux_low = low * (p_low - p + GRAVITY)
        flux_high = high * (p - p_high + GRAVITY)
        source = (flux_x - roll(flux_x, -1, 0)) + (flux_y - roll(flux_y, -1, 1))
        source = source + (flux_low - flux_high) - slab_of(grow, z)
        diagonal = slab_of(stor, z) + (across + roll(across, -1, 0)) + (along + roll(along, -1, 1))
        inverse = 1.0 / (diagonal + (low + high))
        fx[z], fy[z], fz[z + 1] = across, along, high
        src[z], inv[z] = source, inverse
        err[z] = jnp.where(parity0 == (z & 1), source * inverse, 0.0)
        return carry

    lax.fori_loop(2, zw - 2, face_step, 0, unroll=4)

    def sum0(z):
        return neighbour_sum(
            err[z],
            err[z - 1],
            err[z + 1],
            fx[z],
            fy[z],
            fz[z],
            fz[z + 1],
            1,
        )

    def smooth_step(z, carry):
        updated = (src[z] + sum0(z)) * inv[z]
        err[z] = jnp.where(parity0 == (z & 1), err[z], updated)
        return carry

    lax.fori_loop(3, zw - 3, smooth_step, 0, unroll=3)

    def coarse_step(k, carry):
        za, zb = 2 * k, 2 * k + 1
        resid = jnp.where(parity0 == 0, sum0(za), sum0(zb))
        src1[k] = spread_pairs(spread_pairs(resid, x_low, 1, 0), y_low, 1, 1)
        stor1[k] = spread_pairs(
            spread_pairs(slab_of(stor, za) + slab_of(stor, zb), x_low, 1, 0), y_low, 1, 1
        )
        across = spread_pairs(fx[za] + fx[zb], y_low, 1, 1)
        fx1[k] = jnp.where(x_low, across, roll(across, 1, 0))
        along = spread_pairs(fy[za] + fy[zb], x_low, 1, 0)
        fy1[k] = jnp.where(y_low, along, roll(along, 1, 1))
        fz1[k] = spread_pairs(spread_pairs(fz[za], x_low, 1, 0), y_low, 1, 1)
        return carry

    lax.fori_loop(2, zw // 2 - 1, coarse_step, 0, unroll=3)

    def first1(k, carry):
        across, along = fx1[k], fy1[k]
        diagonal = stor1[k] + (across + roll(across, -2, 0)) + (along + roll(along, -2, 1))
        inverse = 1.0 / (diagonal + (fz1[k] + fz1[k + 1]))
        inv1[k] = inverse
        err1[k] = jnp.where(parity1 == (k & 1), src1[k] * inverse, 0.0)
        return carry

    low1, high1 = zl // 2 - 2, zl + 2
    lax.fori_loop(low1, high1, first1, 0, unroll=4)

    def sum1(k):
        return neighbour_sum(
            err1[k], err1[k - 1], err1[k + 1], fx1[k], fy1[k], fz1[k], fz1[k + 1], 2
        )

    def second1(k, carry):
        updated = (src1[k] + sum1(k)) * inv1[k]
        err1[k] = jnp.where(parity1 == (k & 1), err1[k], updated)
        return carry

    lax.fori_loop(low1 + 1, high1 - 1, second1, 0, unroll=3)

    rows2[...] = jnp.zeros(rows2.shape, jnp.float32)
    own1 = zl // 2
    for k2 in range(zl // 4):
        ka, kb = own1 + 2 * k2, own1 + 2 * k2 + 1
        resid = jnp.where(parity1 == 0, sum1(ka), sum1(kb))
        terms = (
            spread_pairs(spread_pairs(resid, x_low2, 2, 0), y_low2, 2, 1),
            spread_pairs(spread_pairs(stor1[ka] + stor1[kb], x_low2, 2, 0), y_low2, 2, 1),
            spread_pairs(fx1[ka] + fx1[kb], y_low2, 2, 1),
            spread_pairs(fy1[ka] + fy1[kb], x_low2, 2, 0),
            spread_pairs(spread_pairs(fz1[ka], x_low2, 2, 0), y_low2, 2, 1),
        )
        for t, term in enumerate(terms):
            for x2 in range(xl // 4):
                at = (t * (xl // 4) + x2) * (zl // 4) + k2
                x = xl + 4 * x2
                rows2[at : at + 1, :] = term[x : x + 1, :]
    pick_shape = (ny, ny // 4)
    pick = lax.broadcasted_iota(jnp.int32, pick_shape, 0) == 4 * lax.broadcasted_iota(
        jnp.int32, pick_shape, 1
    )
    payload_ref[0 : rows2.shape[0], :] = jnp.dot(
        rows2[...], jnp.where(pick, 1.0, 0.0), precision=HI, preferred_element_type=jnp.float32
    )
    own = slice(xl, 2 * xl)
    here = [err1[own1 + k][own] for k in range(4)]
    xo, yo = x_low[own], y_low[own]
    plane = jnp.where(xo, jnp.where(yo, here[0], here[1]), jnp.where(yo, here[2], here[3]))
    base = rows2.shape[0]
    for c in range(ny // 128):
        payload_ref[base + 8 * c : base + 8 * c + 8, :] = plane[:, 128 * c : 128 * c + 128]

    def keep0(i, carry):
        for out, ref in zip(outs0, (err, src, inv, fx, fy, fz)):
            out[i] = ref[zl - 2 + i]
        return carry

    lax.fori_loop(0, zl + 4, keep0, 0, unroll=3)

    def keep1(i, carry):
        for out, ref in zip(outs1, (src1, inv1, fx1, fy1, fz1)):
            out[i] = ref[zl // 2 - 2 + i]
        return carry

    lax.fori_loop(0, zl // 2 + 5, keep1, 0, unroll=3)


def solve_blocks(block, factors, answer, strips, slabs):
    zero = jnp.zeros((1, 128), jnp.float32)

    def entry(kind, b, z):
        return block[kind, b, 2 * z : 2 * z + 1, :]

    pairs = [(i, j) for i in range(slabs) for j in range(i, slabs)]

    def forward(b, carry):
        a = dict(zip(pairs, carry[: len(pairs)]))
        r = list(carry[len(pairs) :]) + [zero] * slabs
        for z in range(slabs):
            here, after = entry(2, b, z), entry(2, b + 1, z)
            low = entry(3, b, z)
            high = entry(3, b, z + 1) if z + 1 < slabs else zero
            a[z, z] = a[z, z] + (entry(1, b, z) + here + after + low + high)
            if z + 1 < slabs:
                a[z, z + 1] = a[z, z + 1] - high
            a[z, slabs + z] = -after
            r[z] = r[z] + entry(0, b, z)
        for i in range(slabs):
            inverse = 1.0 / a[i, i]
            others = list(range(i + 1, slabs + i + 1))
            scaled = [a[i, j] * inverse if (i, j) in a else None for j in others]
            for n, j in enumerate(others):
                if scaled[n] is None:
                    continue
                for k in others[n:]:
                    if (i, k) in a:
                        a[j, k] = a.get((j, k), zero) - scaled[n] * a[i, k]
                r[j] = r[j] - scaled[n] * r[i]
                factors[b, i * (slabs + 1) + n] = scaled[n]
            factors[b, i * (slabs + 1) + slabs] = r[i] * inverse
        nexts = [a.get((slabs + i, slabs + j), zero) for i, j in pairs]
        return tuple(nexts + r[slabs:])

    unroll = strips if strips <= 8 else 1
    lax.fori_loop(0, strips, forward, (zero,) * (len(pairs) + slabs), unroll=unroll)

    def backward(n, above):
        b = strips - 1 - n
        x = [None] * slabs + list(above)
        for i in reversed(range(slabs)):
            value = factors[b, i * (slabs + 1) + slabs]
            for n, j in enumerate(range(i + 1, slabs + i + 1)):
                value = value - factors[b, i * (slabs + 1) + n] * x[j]
            x[i] = value
            answer[b, 2 * i : 2 * i + 2, :] = jnp.broadcast_to(value, (2, 128))
        return tuple(x[:slabs])

    lax.fori_loop(0, strips, backward, (zero,) * slabs, unroll=unroll)


def up_kernel(slabs, strips, zl, xl, counts, *refs):
    where_ref, refs = refs[0], refs[1:]
    pieces, refs = refs[: len(counts)], refs[len(counts) :]
    near, refs = refs[:3], refs[3:]
    e0_in, src0, inv0, fx0, fy0, fz0 = refs[:6]
    src1, inv1, fx1, fy1, fz1 = refs[6:11]
    head_ref, out_ref = refs[11], refs[12]
    a2, block, factors, answer, e2, picked, wide, e1, e0 = refs[13:]
    strip, slab = where_ref[0], where_ref[1]
    x2, z2 = xl // 4, zl // 4
    rows2 = strips * x2
    ny = head_ref.shape[2]

    index = 0
    for ref, count in zip(pieces, counts):
        for j in range(count):
            at = jnp.bitwise_xor(strip, index)
            for g in range(slabs):
                piece = ref[j, jnp.bitwise_xor(slab, g)]
                for t in range(5):
                    for x in range(x2):
                        k = (t * x2 + x) * z2
                        a2[t, at * x2 + x, g * z2 : g * z2 + z2, :] = piece[k : k + z2, :]
            index += 1

    shape = (rows2, 8, 128)
    source, store, fx, fy, fz = (a2[t] for t in range(5))

    def shift_x(v, step):
        if step > 0:
            return jnp.concatenate([jnp.zeros_like(v[:1]), v[:-1]], axis=0)
        return jnp.concatenate([v[1:], jnp.zeros_like(v[:1])], axis=0)

    def along(v, step, axis):
        return pltpu.roll(v, step % v.shape[axis], axis)

    fx_up, fy_up, fz_up = shift_x(fx, -1), along(fy, -1, 2), along(fz, -1, 1)
    inverse = 1.0 / (store + (fx + fx_up) + (fy + fy_up) + (fz + fz_up))
    parity = (
        lax.broadcasted_iota(jnp.int32, shape, 0)
        + lax.broadcasted_iota(jnp.int32, shape, 1)
        + lax.broadcasted_iota(jnp.int32, shape, 2)
    ) & 1
    even = parity == 0

    def sum2(e):
        total = fx * shift_x(e, 1) + fx_up * shift_x(e, -1)
        total = total + (fy * along(e, 1, 2) + fy_up * along(e, -1, 2))
        return total + (fz * along(e, 1, 1) + fz_up * along(e, -1, 1))

    e = jnp.where(even, source * inverse, 0.0)
    e = jnp.where(even, e, (source + sum2(e)) * inverse)
    resid = jnp.where(even, sum2(e), 0.0)

    def blocks(v, both_rows, both_layers):
        v = v.reshape(strips, x2, 8, 128)
        v = v[:, 0] + v[:, 1] if both_rows else v[:, 0]
        v = jnp.sum(v, axis=2, keepdims=True)
        v = jnp.broadcast_to(v, (strips, 8, 128))
        return v + along(v, -1, 1) if both_layers else v

    block[0, 0:strips] = blocks(resid, True, True)
    block[1, 0:strips] = blocks(store, True, True)
    block[2, 0:strips] = blocks(fx, False, True)
    block[2, strips] = jnp.zeros((8, 128), jnp.float32)
    block[3, 0:strips] = blocks(fz, True, False)
    solve_blocks(block, factors, answer, strips, slabs)
    add = jnp.broadcast_to(answer[...][:, None], (strips, x2, 8, 128)).reshape(shape)
    e = e + add
    e = jnp.where(even, (source + sum2(e)) * inverse, e)
    e = jnp.where(even, e, (source + sum2(e)) * inverse)
    e2[...] = jnp.zeros(e2.shape, jnp.float32)
    e2[x2 : x2 + rows2, 8:16, :] = e

    picked[...] = jnp.zeros(picked.shape, jnp.float32)
    for z in range(3 * z2):
        for x in range(3 * x2):
            at = z * 3 * x2 + x
            picked[at : at + 1, :] = e2[
                strip * x2 + x, pl.ds(8 - z2 + slab * z2 + z, 1), :
            ]
    spread_shape = (ny // 4, ny)
    spread = lax.broadcasted_iota(jnp.int32, spread_shape, 0) == (
        lax.broadcasted_iota(jnp.int32, spread_shape, 1) >> 2
    )
    wide[...] = jnp.dot(
        picked[...], jnp.where(spread, 1.0, 0.0), precision=HI, preferred_element_type=jnp.float32
    )

    zl1 = zl // 2
    small = (xl, ny)
    xo = (lax.broadcasted_iota(jnp.int32, small, 0) & 1) == 0
    yo = (lax.broadcasted_iota(jnp.int32, small, 1) & 1) == 0
    for zb in range(3):
        g = slab + (zb - 1)
        inside = jnp.logical_and(g >= 0, g < slabs)
        m = jnp.bitwise_xor(slab, jnp.clip(g, 0, slabs - 1))
        keep = jnp.where(inside, 1.0, 0.0)
        for which in range(3):
            xb = place(which, strip)
            tile = near[which][m]
            plane = jnp.concatenate(
                [tile[8 * c : 8 * c + 8, :] for c in range(ny // 128)], axis=1
            )
            plane = plane * keep
            for k in range(4):
                xk, yk = k // 2, k % 2
                v = jnp.where(jnp.logical_and(xo == (xk == 0), yo == (yk == 0)), plane, 0.0)
                v = v + roll(v, 1 if xk == 0 else -1, 0)
                v = v + roll(v, 1 if yk == 0 else -1, 1)
                e1[zb * zl1 + k, xb] = v
    window = (3 * xl, ny)
    for k in range(3 * zl1):
        rows = [wide[k // 2 * 3 * x2 + x : k // 2 * 3 * x2 + x + 1, :] for x in range(3 * x2)]
        rows = [jnp.broadcast_to(row, (4, ny)) for row in rows]
        rows = [jnp.concatenate(rows[x2 * b : x2 * b + x2], axis=0)[None] for b in range(3)]
        e1[k] = e1[k] + jnp.concatenate(rows, axis=0)

    def at1(k):
        return e1[k].reshape(window)

    xi = lax.broadcasted_iota(jnp.int32, window, 0)
    yi = lax.broadcasted_iota(jnp.int32, window, 1)
    parity0 = (xi + yi) & 1
    parity1 = ((xi >> 1) + (yi >> 1)) & 1

    def level1(k, colour):
        i = k - (zl1 - 2)
        total = neighbour_sum(
            at1(k), at1(k - 1), at1(k + 1), fx1[i], fy1[i], fz1[i], fz1[i + 1], 2
        )
        updated = (src1[i] + total) * inv1[i]
        e1[k] = jnp.where(parity1 == ((k + colour) & 1), updated, at1(k)).reshape(3, xl, ny)

    def up1(colour, reach):
        def step(k, carry):
            level1(k, colour)
            return carry

        lax.fori_loop(zl1 - reach, 2 * zl1 + reach, step, 0, unroll=2)

    up1(0, 2)
    up1(1, 1)

    def join(i, carry):
        e0[i] = e0_in[i] + at1((zl - 2 + i) // 2)
        return carry

    lax.fori_loop(0, zl + 4, join, 0, unroll=3)

    def up0(colour, reach):
        def step(i, carry):
            total = neighbour_sum(
                e0[i], e0[i - 1], e0[i + 1], fx0[i], fy0[i], fz0[i], fz0[i + 1], 1
            )
            updated = (src0[i] + total) * inv0[i]
            e0[i] = jnp.where(parity0 == ((i + colour) & 1), updated, e0[i])
            return carry

        lax.fori_loop(2 - reach, zl + 2 + reach, step, 0, unroll=2)

    up0(0, 1)
    up0(1, 0)
    for z in range(zl):
        out_ref[z] = head_ref[z] + e0[z + 2][xl : 2 * xl]


def lay_kernel(head_ref, soil_ref, land_ref, sun_ref, out_ref):
    zl = head_ref.shape[0]
    out_ref[0:zl] = head_ref[...]
    out_ref[zl : 2 * zl] = soil_ref[...].astype(jnp.float32)
    hour = sun_ref[...].astype(jnp.float32)
    sun_share = jnp.maximum(0.0, jnp.sin(math.pi * (hour - 6.0) / 12.0))
    out_ref[2 * zl] = ET_PEAK * sun_share * land_ref[...].astype(jnp.float32)


VMEM = pl.BlockSpec(memory_space=pltpu.VMEM)
SMEM = pl.BlockSpec(memory_space=pltpu.SMEM)


def f32(*shape):
    return jax.ShapeDtypeStruct(shape, jnp.float32)


def down(first, slabs, strips, zl, xl, ny, where, table, state, head=None, sat_old=None):
    zw, xw = 3 * zl, 3 * xl
    rows2 = 5 * (xl // 4) * (zl // 4)
    rows2 = -(-rows2 // 8) * 8
    out_shape = [f32(rows2 + 8 * ny // 128, 128)]
    out_shape += [f32(zl + 4, xw, ny)] * 6 + [f32(zl // 2 + 5, xw, ny)] * 5
    operands = [where, table, *state]
    if first:
        out_shape.append(f32(zw, 3, xl, ny))
    else:
        operands += [*head, sat_old]
    split = pltpu.VMEM((zw, 3, xl, ny), jnp.float32)
    full, half = pltpu.VMEM((zw, xw, ny), jnp.float32), pltpu.VMEM((zw // 2, xw, ny), jnp.float32)
    tall = pltpu.VMEM((zw + 1, xw, ny), jnp.float32)
    return pl.pallas_call(
        functools.partial(down_kernel, first, slabs, strips, zl, xl),
        out_shape=out_shape,
        in_specs=[SMEM] + [VMEM] * (len(operands) - 1),
        out_specs=[VMEM] * len(out_shape),
        scratch_shapes=[split] * 4 + [full] * 2 + [tall] + [full] * 3 + [half] * 7
        + [pltpu.VMEM((rows2, ny), jnp.float32), pltpu.VMEM((8, 128), jnp.float32)],
        compiler_params=pltpu.CompilerParams(vmem_limit_bytes=44 * 1024 * 1024),
    )(*operands)


def up(slabs, strips, zl, xl, ny, where, pieces, near, kept, head):
    x2, z2 = xl // 4, zl // 4
    counts = [p.shape[0] for p in pieces]
    operands = [where, *pieces, *near, *kept, head]
    n = -(-9 * x2 * z2 // 8) * 8
    scratch = [
        pltpu.VMEM((5, strips * x2, 8, 128), jnp.float32),
        pltpu.VMEM((4, strips + 1, 8, 128), jnp.float32),
        pltpu.VMEM((strips, slabs * (slabs + 1), 1, 128), jnp.float32),
        pltpu.VMEM((strips, 8, 128), jnp.float32),
        pltpu.VMEM(((strips + 2) * x2, 24, 128), jnp.float32),
        pltpu.VMEM((n, ny // 4), jnp.float32),
        pltpu.VMEM((n, ny), jnp.float32),
        pltpu.VMEM((3 * zl // 2, 3, xl, ny), jnp.float32),
        pltpu.VMEM((zl + 4, 3 * xl, ny), jnp.float32),
    ]
    return pl.pallas_call(
        functools.partial(up_kernel, slabs, strips, zl, xl, counts),
        out_shape=f32(zl, xl, ny),
        in_specs=[SMEM] + [VMEM] * (len(operands) - 1),
        out_specs=VMEM,
        scratch_shapes=scratch,
        compiler_params=pltpu.CompilerParams(vmem_limit_bytes=44 * 1024 * 1024),
    )(*operands)


def swapped(x, axis, mask):
    return lax.ppermute(x, axis, [(i, i ^ mask) for i in range(lax.axis_size(axis))])


def odd_pairs(x, axis):
    size = lax.axis_size(axis)
    pairs = [(i, i + 1) for i in range(1, size - 1, 2)]
    return lax.ppermute(x, axis, pairs + [(j, i) for i, j in pairs])


def neighbourhood(x):
    row = [x, swapped(x, "xy", 1), odd_pairs(x, "xy")]
    return row + [swapped(v, "gz", 1) for v in row] + [odd_pairs(v, "gz") for v in row]


def gather_strips(own, partner):
    size = lax.axis_size("xy")
    x = jnp.stack([own, partner])
    if size == 8:
        return [x] + [swapped(x, "xy", m) for m in (2, 4, 6)]
    mask = 2
    while mask < size:
        x = jnp.concatenate([x, swapped(x, "xy", mask)])
        mask *= 2
    return [x]


def per_device(head_old, soil_type, soil_table, land_mask, sun_bin):
    zl, xl, ny = head_old.shape
    strips, slabs = lax.axis_size("xy"), lax.axis_size("gz")
    where = jnp.stack([lax.axis_index("xy"), lax.axis_index("gz")]).astype(jnp.int32)
    own = pl.pallas_call(
        lay_kernel,
        out_shape=f32(2 * zl + 1, xl, ny),
        in_specs=[VMEM] * 4,
        out_specs=VMEM,
    )(head_old, soil_type, land_mask, sun_bin)
    state = neighbourhood(own)
    sizes = (slabs, strips, zl, xl, ny)
    base = -(-5 * (xl // 4) * (zl // 4) // 8) * 8

    def finish(payload, kept, head):
        slab = [payload] + [swapped(payload, "gz", m) for m in range(1, slabs)]
        full = jnp.stack(slab)
        partner = swapped(full, "xy", 1)
        pieces = gather_strips(full[:, :base], partner[:, :base])
        near = [full[:, base:], partner[:, base:], odd_pairs(full[:, base:], "xy")]
        return up(*sizes, where, pieces, near, kept, head)

    payload, *kept, sat_old = down(True, *sizes, where, soil_table, state)
    head = finish(payload, kept, head_old)
    payload, *kept = down(
        False, *sizes, where, soil_table, state, neighbourhood(head), sat_old
    )
    return finish(payload, kept, head)


def solution(mesh):
    in_specs = (P("gz", "xy", None), P("gz", "xy", None), P(), P("xy", None), P("xy", None))
    out_specs = P("gz", "xy", None)
    return jax.shard_map(
        per_device, mesh=mesh, in_specs=in_specs, out_specs=out_specs, check_vma=False
    )
```

```python
import functools
import math

import jax
import jax.numpy as jnp
from jax import lax
from jax.experimental import pallas as pl
from jax.experimental.pallas import tpu as pltpu
from jax.sharding import PartitionSpec as P

DT = 20.0
ET_PEAK = 0.008
GRAVITY = 0.1
ROOT_DECAY = 3.0
HI = lax.Precision.HIGHEST


def roll(value, shift, axis):
    return pltpu.roll(value, shift % value.shape[axis], axis)


def place(which, index):
    if which == 0:
        return 1
    odd = index & 1
    return 2 - 2 * odd if which == 1 else 2 * odd


def spread_pairs(value, low, step, axis):
    return value + jnp.where(low, roll(value, -step, axis), roll(value, step, axis))


def neighbour_sum(e, below, above, fx, fy, fz, fz_up, step):
    total = fx * roll(e, step, 0) + roll(fx * e, -step, 0)
    total = total + (fy * roll(e, step, 1) + roll(fy * e, -step, 1))
    return total + (fz * below + fz_up * above)


def look_up(table, row, index):
    picked = jnp.broadcast_to(table[row : row + 1, :], (8, 128))
    rows = []
    for r in range(0, index.shape[0], 8):
        cols = []
        for c in range(0, index.shape[1], 128):
            at = index[r : r + 8, c : c + 128]
            cols.append(jnp.take_along_axis(picked, at, axis=1, mode="promise_in_bounds"))
        rows.append(jnp.concatenate(cols, axis=1))
    return jnp.concatenate(rows, axis=0)


def down_kernel(first, slabs, strips, zl, xl, *refs):
    where_ref, table_ref = refs[0], refs[1]
    refs = refs[2:]
    state_refs, refs = refs[:9], refs[9:]
    if first:
        head_refs = state_refs
    else:
        head_refs, refs = refs[:9], refs[9:]
        sat_old_ref, refs = refs[0], refs[1:]
    payload_ref, refs = refs[0], refs[1:]
    err, src, inv, fx, fy, fz = refs[:6]
    src1, inv1, fx1, fy1, fz1 = refs[6:11]
    refs = refs[11:]
    if first:
        sat_out, refs = refs[0], refs[1:]
    head, cond, stor, grow, stor1, err1, rows2 = refs

    strip, slab = where_ref[0], where_ref[1]
    zw, xw = 3 * zl, 3 * xl
    ny = head.shape[3]
    shape = (xw, ny)

    def slab_of(ref, z):
        return ref[z].reshape(shape)

    xi = lax.broadcasted_iota(jnp.int32, shape, 0)
    yi = lax.broadcasted_iota(jnp.int32, shape, 1)
    parity0 = (xi + yi) & 1
    parity1 = ((xi >> 1) + (yi >> 1)) & 1
    x_low, y_low = (xi & 1) == 0, (yi & 1) == 0
    x_low2, y_low2 = (xi & 2) == 0, (yi & 2) == 0
    edge_x = jnp.logical_or(
        jnp.logical_and(xi == xl, strip == 0), jnp.logical_and(xi == 2 * xl, strip == strips - 1)
    )
    edge_y = yi == 0

    def edge_z(z, width):
        return jnp.logical_or(
            jnp.logical_and(z == width, slab == 0),
            jnp.logical_and(z == 2 * width, slab == slabs - 1),
        )

    table = table_ref[...]
    for block in range(9):
        z_at, x_at = place(block // 3, slab), place(block % 3, strip)

        def soil_step(i, carry, block=block, z_at=z_at, x_at=x_at):
            z = z_at * zl + i
            soil = state_refs[block][zl + i].astype(jnp.int32)
            p = head_refs[block][i]
            forcing = state_refs[block % 3][2 * zl]
            dtheta, alpha, shape_n, k_sat, expon_m = (look_up(table, k, soil) for k in range(5))
            layer = (slab * zl - zl + z).astype(jnp.float32)
            depth = jnp.full((1, ny), layer, jnp.float32)
            sink = forcing * jnp.exp(-ROOT_DECAY * depth / (slabs * zl))
            log_s = jnp.log(jnp.abs(alpha * p))
            log_p = shape_n * log_s
            log_b = jnp.log(1.0 + jnp.exp(log_p))
            root = jnp.exp(-0.5 * expon_m * log_b)
            sat = root * root
            slope = expon_m * shape_n * alpha * sat * jnp.exp((shape_n - 1.0) * log_s - log_b)
            cond[z, x_at] = k_sat * root * jnp.square(1.0 - jnp.exp(expon_m * (log_p - log_b)))
            stor[z, x_at] = slope * (dtheta / DT + sink)
            g = sink * sat
            if first:
                sat_out[z, x_at] = sat
            else:
                g = g + dtheta * (sat - sat_old_ref[z, x_at]) / DT
            grow[z, x_at] = g
            head[z, x_at] = p
            return carry

        skip = 0 if block < 3 else 1
        start = jnp.where(z_at == 0, skip, 0)
        lax.fori_loop(0, zl - skip, lambda i, c: soil_step(start + i, c), 0, unroll=zl - skip)

    def face_z(z):
        both = 0.5 * (slab_of(cond, z - 1) + slab_of(cond, z))
        return both * jnp.where(edge_z(z, zl), 0.0, 1.0)

    fz[2] = face_z(2)

    def face_step(z, carry):
        c, p = slab_of(cond, z), slab_of(head, z)
        across = jnp.where(edge_x, 0.0, 0.5 * (c + roll(c, 1, 0)))
        along = jnp.where(edge_y, 0.0, 0.5 * (c + roll(c, 1, 1)))
        low, high = fz[z], face_z(z + 1)
        flux_x = across * (roll(p, 1, 0) - p)
        flux_y = along * (roll(p, 1, 1) - p)
        p_low = slab_of(head, z - 1)
        p_high = slab_of(head, z + 1)
        flux_low = low * (p_low - p + GRAVITY)
        flux_high = high * (p - p_high + GRAVITY)
        source = (flux_x - roll(flux_x, -1, 0)) + (flux_y - roll(flux_y, -1, 1))
        source = source + (flux_low - flux_high) - slab_of(grow, z)
        diagonal = slab_of(stor, z) + (across + roll(across, -1, 0)) + (along + roll(along, -1, 1))
        inverse = 1.0 / (diagonal + (low + high))
        fx[z], fy[z], fz[z + 1] = across, along, high
        src[z], inv[z] = source, inverse
        err[z] = jnp.where(parity0 == (z & 1), source * inverse, 0.0)
        return carry

    lax.fori_loop(2, zw - 2, face_step, 0, unroll=4)

    def sum0(z):
        return neighbour_sum(
            err[z],
            err[z - 1],
            err[z + 1],
            fx[z],
            fy[z],
            fz[z],
            fz[z + 1],
            1,
        )

    def smooth_step(z, carry):
        updated = (src[z] + sum0(z)) * inv[z]
        err[z] = jnp.where(parity0 == (z & 1), err[z], updated)
        return carry

    lax.fori_loop(3, zw - 3, smooth_step, 0, unroll=3)

    def coarse_step(k, carry):
        za, zb = 2 * k, 2 * k + 1
        resid = jnp.where(parity0 == 0, sum0(za), sum0(zb))
        src1[k] = spread_pairs(spread_pairs(resid, x_low, 1, 0), y_low, 1, 1)
        stor1[k] = spread_pairs(
            spread_pairs(slab_of(stor, za) + slab_of(stor, zb), x_low, 1, 0), y_low, 1, 1
        )
        across = spread_pairs(fx[za] + fx[zb], y_low, 1, 1)
        fx1[k] = jnp.where(x_low, across, roll(across, 1, 0))
        along = spread_pairs(fy[za] + fy[zb], x_low, 1, 0)
        fy1[k] = jnp.where(y_low, along, roll(along, 1, 1))
        fz1[k] = spread_pairs(spread_pairs(fz[za], x_low, 1, 0), y_low, 1, 1)
        return carry

    lax.fori_loop(2, zw // 2 - 1, coarse_step, 0, unroll=3)

    def first1(k, carry):
        across, along = fx1[k], fy1[k]
        diagonal = stor1[k] + (across + roll(across, -2, 0)) + (along + roll(along, -2, 1))
        inverse = 1.0 / (diagonal + (fz1[k] + fz1[k + 1]))
        inv1[k] = inverse
        err1[k] = jnp.where(parity1 == (k & 1), src1[k] * inverse, 0.0)
        return carry

    low1, high1 = zl // 2 - 2, zl + 2
    lax.fori_loop(low1, high1, first1, 0, unroll=4)

    def sum1(k):
        return neighbour_sum(
            err1[k], err1[k - 1], err1[k + 1], fx1[k], fy1[k], fz1[k], fz1[k + 1], 2
        )

    def second1(k, carry):
        updated = (src1[k] + sum1(k)) * inv1[k]
        err1[k] = jnp.where(parity1 == (k & 1), err1[k], updated)
        return carry

    lax.fori_loop(low1 + 1, high1 - 1, second1, 0, unroll=3)

    rows2[...] = jnp.zeros(rows2.shape, jnp.float32)
    own1 = zl // 2
    for k2 in range(zl // 4):
        ka, kb = own1 + 2 * k2, own1 + 2 * k2 + 1
        resid = jnp.where(parity1 == 0, sum1(ka), sum1(kb))
        terms = (
            spread_pairs(spread_pairs(resid, x_low2, 2, 0), y_low2, 2, 1),
            spread_pairs(spread_pairs(stor1[ka] + stor1[kb], x_low2, 2, 0), y_low2, 2, 1),
            spread_pairs(fx1[ka] + fx1[kb], y_low2, 2, 1),
            spread_pairs(fy1[ka] + fy1[kb], x_low2, 2, 0),
            spread_pairs(spread_pairs(fz1[ka], x_low2, 2, 0), y_low2, 2, 1),
        )
        for t, term in enumerate(terms):
            for x2 in range(xl // 4):
                at = (t * (xl // 4) + x2) * (zl // 4) + k2
                x = xl + 4 * x2
                rows2[at : at + 1, :] = term[x : x + 1, :]
    pick_shape = (ny, ny // 4)
    pick = lax.broadcasted_iota(jnp.int32, pick_shape, 0) == 4 * lax.broadcasted_iota(
        jnp.int32, pick_shape, 1
    )
    payload_ref[0 : rows2.shape[0], :] = jnp.dot(
        rows2[...], jnp.where(pick, 1.0, 0.0), precision=HI, preferred_element_type=jnp.float32
    )
    own = slice(xl, 2 * xl)
    here = [err1[own1 + k][own] for k in range(4)]
    xo, yo = x_low[own], y_low[own]
    plane = jnp.where(xo, jnp.where(yo, here[0], here[1]), jnp.where(yo, here[2], here[3]))
    base = rows2.shape[0]
    for c in range(ny // 128):
        payload_ref[base + 8 * c : base + 8 * c + 8, :] = plane[:, 128 * c : 128 * c + 128]


def solve_blocks(block, factors, answer, strips, slabs):
    zero = jnp.zeros((1, 128), jnp.float32)

    def entry(kind, b, z):
        return block[kind, b, 2 * z : 2 * z + 1, :]

    pairs = [(i, j) for i in range(slabs) for j in range(i, slabs)]

    def forward(b, carry):
        a = dict(zip(pairs, carry[: len(pairs)]))
        r = list(carry[len(pairs) :]) + [zero] * slabs
        for z in range(slabs):
            here, after = entry(2, b, z), entry(2, b + 1, z)
            low = entry(3, b, z)
            high = entry(3, b, z + 1) if z + 1 < slabs else zero
            a[z, z] = a[z, z] + (entry(1, b, z) + here + after + low + high)
            if z + 1 < slabs:
                a[z, z + 1] = a[z, z + 1] - high
            a[z, slabs + z] = -after
            r[z] = r[z] + entry(0, b, z)
        for i in range(slabs):
            inverse = 1.0 / a[i, i]
            others = list(range(i + 1, slabs + i + 1))
            scaled = [a[i, j] * inverse if (i, j) in a else None for j in others]
            for n, j in enumerate(others):
                if scaled[n] is None:
                    continue
                for k in others[n:]:
                    if (i, k) in a:
                        a[j, k] = a.get((j, k), zero) - scaled[n] * a[i, k]
                r[j] = r[j] - scaled[n] * r[i]
                factors[b, i * (slabs + 1) + n] = scaled[n]
            factors[b, i * (slabs + 1) + slabs] = r[i] * inverse
        nexts = [a.get((slabs + i, slabs + j), zero) for i, j in pairs]
        return tuple(nexts + r[slabs:])

    unroll = strips if strips <= 8 else 1
    lax.fori_loop(0, strips, forward, (zero,) * (len(pairs) + slabs), unroll=unroll)

    def backward(n, above):
        b = strips - 1 - n
        x = [None] * slabs + list(above)
        for i in reversed(range(slabs)):
            value = factors[b, i * (slabs + 1) + slabs]
            for n, j in enumerate(range(i + 1, slabs + i + 1)):
                value = value - factors[b, i * (slabs + 1) + n] * x[j]
            x[i] = value
            answer[b, 2 * i : 2 * i + 2, :] = jnp.broadcast_to(value, (2, 128))
        return tuple(x[:slabs])

    lax.fori_loop(0, strips, backward, (zero,) * slabs, unroll=unroll)


def up_kernel(slabs, strips, zl, xl, counts, *refs):
    where_ref, refs = refs[0], refs[1:]
    pieces, refs = refs[: len(counts)], refs[len(counts) :]
    near, refs = refs[:3], refs[3:]
    e0_in, src0, inv0, fx0, fy0, fz0 = refs[:6]
    src1, inv1, fx1, fy1, fz1 = refs[6:11]
    head_ref, out_ref = refs[11], refs[12]
    a2, block, factors, answer, e2, picked, wide, e1, e0 = refs[13:]
    strip, slab = where_ref[0], where_ref[1]
    x2, z2 = xl // 4, zl // 4
    rows2 = strips * x2
    ny = head_ref.shape[2]

    index = 0
    for ref, count in zip(pieces, counts):
        for j in range(count):
            at = jnp.bitwise_xor(strip, index)
            for g in range(slabs):
                piece = ref[j, jnp.bitwise_xor(slab, g)]
                for t in range(5):
                    for x in range(x2):
                        k = (t * x2 + x) * z2
                        a2[t, at * x2 + x, g * z2 : g * z2 + z2, :] = piece[k : k + z2, :]
            index += 1

    shape = (rows2, 8, 128)
    source, store, fx, fy, fz = (a2[t] for t in range(5))

    def shift_x(v, step):
        if step > 0:
            return jnp.concatenate([jnp.zeros_like(v[:1]), v[:-1]], axis=0)
        return jnp.concatenate([v[1:], jnp.zeros_like(v[:1])], axis=0)

    def along(v, step, axis):
        return pltpu.roll(v, step % v.shape[axis], axis)

    fx_up, fy_up, fz_up = shift_x(fx, -1), along(fy, -1, 2), along(fz, -1, 1)
    inverse = 1.0 / (store + (fx + fx_up) + (fy + fy_up) + (fz + fz_up))
    parity = (
        lax.broadcasted_iota(jnp.int32, shape, 0)
        + lax.broadcasted_iota(jnp.int32, shape, 1)
        + lax.broadcasted_iota(jnp.int32, shape, 2)
    ) & 1
    even = parity == 0

    def sum2(e):
        total = fx * shift_x(e, 1) + fx_up * shift_x(e, -1)
        total = total + (fy * along(e, 1, 2) + fy_up * along(e, -1, 2))
        return total + (fz * along(e, 1, 1) + fz_up * along(e, -1, 1))

    e = jnp.where(even, source * inverse, 0.0)
    e = jnp.where(even, e, (source + sum2(e)) * inverse)
    resid = jnp.where(even, sum2(e), 0.0)

    def blocks(v, both_rows, both_layers):
        v = v.reshape(strips, x2, 8, 128)
        v = v[:, 0] + v[:, 1] if both_rows else v[:, 0]
        v = jnp.sum(v, axis=2, keepdims=True)
        v = jnp.broadcast_to(v, (strips, 8, 128))
        return v + along(v, -1, 1) if both_layers else v

    block[0, 0:strips] = blocks(resid, True, True)
    block[1, 0:strips] = blocks(store, True, True)
    block[2, 0:strips] = blocks(fx, False, True)
    block[2, strips] = jnp.zeros((8, 128), jnp.float32)
    block[3, 0:strips] = blocks(fz, True, False)
    solve_blocks(block, factors, answer, strips, slabs)
    add = jnp.broadcast_to(answer[...][:, None], (strips, x2, 8, 128)).reshape(shape)
    e = e + add
    e = jnp.where(even, (source + sum2(e)) * inverse, e)
    e = jnp.where(even, e, (source + sum2(e)) * inverse)
    e2[...] = jnp.zeros(e2.shape, jnp.float32)
    e2[x2 : x2 + rows2, 8:16, :] = e

    picked[...] = jnp.zeros(picked.shape, jnp.float32)
    for z in range(3 * z2):
        for x in range(3 * x2):
            at = z * 3 * x2 + x
            picked[at : at + 1, :] = e2[
                strip * x2 + x, pl.ds(8 - z2 + slab * z2 + z, 1), :
            ]
    spread_shape = (ny // 4, ny)
    spread = lax.broadcasted_iota(jnp.int32, spread_shape, 0) == (
        lax.broadcasted_iota(jnp.int32, spread_shape, 1) >> 2
    )
    wide[...] = jnp.dot(
        picked[...], jnp.where(spread, 1.0, 0.0), precision=HI, preferred_element_type=jnp.float32
    )

    zl1 = zl // 2
    small = (xl, ny)
    xo = (lax.broadcasted_iota(jnp.int32, small, 0) & 1) == 0
    yo = (lax.broadcasted_iota(jnp.int32, small, 1) & 1) == 0
    for zb in range(3):
        g = slab + (zb - 1)
        inside = jnp.logical_and(g >= 0, g < slabs)
        m = jnp.bitwise_xor(slab, jnp.clip(g, 0, slabs - 1))
        keep = jnp.where(inside, 1.0, 0.0)
        for which in range(3):
            xb = place(which, strip)
            tile = near[which][m]
            plane = jnp.concatenate(
                [tile[8 * c : 8 * c + 8, :] for c in range(ny // 128)], axis=1
            )
            plane = plane * keep
            for k in range(4):
                xk, yk = k // 2, k % 2
                v = jnp.where(jnp.logical_and(xo == (xk == 0), yo == (yk == 0)), plane, 0.0)
                v = v + roll(v, 1 if xk == 0 else -1, 0)
                v = v + roll(v, 1 if yk == 0 else -1, 1)
                e1[zb * zl1 + k, xb] = v
    window = (3 * xl, ny)
    for k in range(3 * zl1):
        rows = [wide[k // 2 * 3 * x2 + x : k // 2 * 3 * x2 + x + 1, :] for x in range(3 * x2)]
        rows = [jnp.broadcast_to(row, (4, ny)) for row in rows]
        rows = [jnp.concatenate(rows[x2 * b : x2 * b + x2], axis=0)[None] for b in range(3)]
        e1[k] = e1[k] + jnp.concatenate(rows, axis=0)

    def at1(k):
        return e1[k].reshape(window)

    xi = lax.broadcasted_iota(jnp.int32, window, 0)
    yi = lax.broadcasted_iota(jnp.int32, window, 1)
    parity0 = (xi + yi) & 1
    parity1 = ((xi >> 1) + (yi >> 1)) & 1

    def level1(k, colour):
        total = neighbour_sum(
            at1(k), at1(k - 1), at1(k + 1), fx1[k], fy1[k], fz1[k], fz1[k + 1], 2
        )
        updated = (src1[k] + total) * inv1[k]
        e1[k] = jnp.where(parity1 == ((k + colour) & 1), updated, at1(k)).reshape(3, xl, ny)

    def up1(colour, reach):
        def step(k, carry):
            level1(k, colour)
            return carry

        lax.fori_loop(zl1 - reach, 2 * zl1 + reach, step, 0, unroll=2)

    up1(0, 2)
    up1(1, 1)

    def join(i, carry):
        e0[i] = e0_in[i + zl - 2] + at1((zl - 2 + i) // 2)
        return carry

    lax.fori_loop(0, zl + 4, join, 0, unroll=3)

    def up0(colour, reach):
        def step(i, carry):
            z = i + zl - 2
            total = neighbour_sum(
                e0[i], e0[i - 1], e0[i + 1], fx0[z], fy0[z], fz0[z], fz0[z + 1], 1
            )
            updated = (src0[z] + total) * inv0[z]
            e0[i] = jnp.where(parity0 == ((i + colour) & 1), updated, e0[i])
            return carry

        lax.fori_loop(2 - reach, zl + 2 + reach, step, 0, unroll=2)

    up0(0, 1)
    up0(1, 0)
    for z in range(zl):
        out_ref[z] = head_ref[z] + e0[z + 2][xl : 2 * xl]


VMEM = pl.BlockSpec(memory_space=pltpu.VMEM)
SMEM = pl.BlockSpec(memory_space=pltpu.SMEM)


def f32(*shape):
    return jax.ShapeDtypeStruct(shape, jnp.float32)


def down(first, slabs, strips, zl, xl, ny, where, table, state, head=None, sat_old=None):
    zw, xw = 3 * zl, 3 * xl
    rows2 = 5 * (xl // 4) * (zl // 4)
    rows2 = -(-rows2 // 8) * 8
    out_shape = [f32(rows2 + 8 * ny // 128, 128)]
    out_shape += [f32(zw, xw, ny)] * 6 + [f32(zw // 2, xw, ny)] * 5
    operands = [where, table, *state]
    if first:
        out_shape.append(f32(zw, 3, xl, ny))
    else:
        operands += [*head, sat_old]
    split = pltpu.VMEM((zw, 3, xl, ny), jnp.float32)
    half = pltpu.VMEM((zw // 2, xw, ny), jnp.float32)
    return pl.pallas_call(
        functools.partial(down_kernel, first, slabs, strips, zl, xl),
        out_shape=out_shape,
        in_specs=[SMEM] + [VMEM] * (len(operands) - 1),
        out_specs=[VMEM] * len(out_shape),
        scratch_shapes=[split] * 4 + [half] * 2 + [pltpu.VMEM((rows2, ny), jnp.float32)],
        compiler_params=pltpu.CompilerParams(vmem_limit_bytes=30 * 1024 * 1024),
    )(*operands)


def up(slabs, strips, zl, xl, ny, where, pieces, near, kept, head):
    x2, z2 = xl // 4, zl // 4
    counts = [p.shape[0] for p in pieces]
    operands = [where, *pieces, *near, *kept, head]
    n = -(-9 * x2 * z2 // 8) * 8
    scratch = [
        pltpu.VMEM((5, strips * x2, 8, 128), jnp.float32),
        pltpu.VMEM((4, strips + 1, 8, 128), jnp.float32),
        pltpu.VMEM((strips, slabs * (slabs + 1), 1, 128), jnp.float32),
        pltpu.VMEM((strips, 8, 128), jnp.float32),
        pltpu.VMEM(((strips + 2) * x2, 24, 128), jnp.float32),
        pltpu.VMEM((n, ny // 4), jnp.float32),
        pltpu.VMEM((n, ny), jnp.float32),
        pltpu.VMEM((3 * zl // 2, 3, xl, ny), jnp.float32),
        pltpu.VMEM((zl + 4, 3 * xl, ny), jnp.float32),
    ]
    return pl.pallas_call(
        functools.partial(up_kernel, slabs, strips, zl, xl, counts),
        out_shape=f32(zl, xl, ny),
        in_specs=[SMEM] + [VMEM] * (len(operands) - 1),
        out_specs=VMEM,
        scratch_shapes=scratch,
        compiler_params=pltpu.CompilerParams(vmem_limit_bytes=30 * 1024 * 1024),
    )(*operands)


def swapped(x, axis, mask):
    return lax.ppermute(x, axis, [(i, i ^ mask) for i in range(lax.axis_size(axis))])


def odd_pairs(x, axis):
    size = lax.axis_size(axis)
    pairs = [(i, i + 1) for i in range(1, size - 1, 2)]
    return lax.ppermute(x, axis, pairs + [(j, i) for i, j in pairs])


def neighbourhood(x):
    row = [x, swapped(x, "xy", 1), odd_pairs(x, "xy")]
    return row + [swapped(v, "gz", 1) for v in row] + [odd_pairs(v, "gz") for v in row]


def gather_strips(own, partner):
    size = lax.axis_size("xy")
    x = jnp.stack([own, partner])
    if size == 8:
        return [x] + [swapped(x, "xy", m) for m in (2, 4, 6)]
    mask = 2
    while mask < size:
        x = jnp.concatenate([x, swapped(x, "xy", mask)])
        mask *= 2
    return [x]


def per_device(head_old, soil_type, soil_table, land_mask, sun_bin):
    zl, xl, ny = head_old.shape
    strips, slabs = lax.axis_size("xy"), lax.axis_size("gz")
    where = jnp.stack([lax.axis_index("xy"), lax.axis_index("gz")]).astype(jnp.int32)
    resid, sat, alpha, shape_n, k_sat = soil_table
    table = jnp.stack([sat - resid, alpha, shape_n, k_sat, 1.0 - 1.0 / shape_n])
    table = jnp.pad(table, ((0, 3), (0, 128 - table.shape[1])))
    sun_share = jnp.maximum(0.0, jnp.sin(math.pi * (sun_bin.astype(jnp.float32) - 6.0) / 12.0))
    forcing = ET_PEAK * sun_share * land_mask.astype(jnp.float32)
    across = ((0, 0), (0, 0))
    soil = jnp.pad(soil_type, ((zl, 1), *across)).astype(jnp.float32)
    own = jnp.pad(head_old, ((0, zl + 1), *across)) + soil
    own = own + jnp.pad(forcing[None], ((2 * zl, 0), *across))
    state = neighbourhood(own)
    sizes = (slabs, strips, zl, xl, ny)
    base = -(-5 * (xl // 4) * (zl // 4) // 8) * 8

    def finish(payload, kept, head):
        slab = [payload] + [swapped(payload, "gz", m) for m in range(1, slabs)]
        full = jnp.stack(slab)
        partner = swapped(full, "xy", 1)
        pieces = gather_strips(full[:, :base], partner[:, :base])
        near = [full[:, base:], partner[:, base:], odd_pairs(full[:, base:], "xy")]
        return up(*sizes, where, pieces, near, kept, head)

    payload, *kept, sat_old = down(True, *sizes, where, table, state)
    head = finish(payload, kept, head_old)
    payload, *kept = down(
        False, *sizes, where, table, state, neighbourhood(head), sat_old
    )
    return finish(payload, kept, head)


def solution(mesh):
    in_specs = (P("gz", "xy", None), P("gz", "xy", None), P(), P("xy", None), P("xy", None))
    out_specs = P("gz", "xy", None)
    return jax.shard_map(
        per_device, mesh=mesh, in_specs=in_specs, out_specs=out_specs, check_vma=False
    )
```

```python
import functools
import math

import jax
import jax.numpy as jnp
from jax import lax
from jax.experimental import pallas as pl
from jax.experimental.pallas import tpu as pltpu
from jax.sharding import PartitionSpec as P

DT = 20.0
ET_PEAK = 0.008
GRAVITY = 0.1
ROOT_DECAY = 3.0
HI = lax.Precision.HIGHEST


def roll(value, shift, axis):
    return pltpu.roll(value, shift % value.shape[axis], axis)


def place(which, index):
    if which == 0:
        return 1
    odd = index & 1
    return 2 - 2 * odd if which == 1 else 2 * odd


def spread_pairs(value, low, step, axis):
    return value + jnp.where(low, roll(value, -step, axis), roll(value, step, axis))


def neighbour_sum(e, below, above, fx, fy, fz, fz_up, step):
    total = fx * roll(e, step, 0) + roll(fx * e, -step, 0)
    total = total + (fy * roll(e, step, 1) + roll(fy * e, -step, 1))
    return total + (fz * below + fz_up * above)


def look_up(table, row, index):
    picked = jnp.broadcast_to(table[row : row + 1, :], (8, 128))
    rows = []
    for r in range(0, index.shape[0], 8):
        cols = []
        for c in range(0, index.shape[1], 128):
            at = index[r : r + 8, c : c + 128]
            cols.append(jnp.take_along_axis(picked, at, axis=1, mode="promise_in_bounds"))
        rows.append(jnp.concatenate(cols, axis=1))
    return jnp.concatenate(rows, axis=0)


def down_kernel(first, slabs, strips, zl, xl, *refs):
    where_ref, table_ref = refs[0], refs[1]
    refs = refs[2:]
    state_refs, refs = refs[:9], refs[9:]
    if first:
        head_refs = state_refs
    else:
        head_refs, refs = refs[:9], refs[9:]
        sat_old_ref, refs = refs[0], refs[1:]
    payload_ref, refs = refs[0], refs[1:]
    err, src, inv, fx, fy, fz = refs[:6]
    src1, inv1, fx1, fy1, fz1 = refs[6:11]
    refs = refs[11:]
    if first:
        sat_out, refs = refs[0], refs[1:]
    head, cond, stor, grow, stor1, err1, rows2 = refs

    strip, slab = where_ref[0], where_ref[1]
    zw, xw = 3 * zl, 3 * xl
    ny = head.shape[3]
    shape = (xw, ny)

    def slab_of(ref, z):
        return ref[z].reshape(shape)

    xi = lax.broadcasted_iota(jnp.int32, shape, 0)
    yi = lax.broadcasted_iota(jnp.int32, shape, 1)
    parity0 = (xi + yi) & 1
    parity1 = ((xi >> 1) + (yi >> 1)) & 1
    x_low, y_low = (xi & 1) == 0, (yi & 1) == 0
    x_low2, y_low2 = (xi & 2) == 0, (yi & 2) == 0
    edge_x = jnp.logical_or(
        jnp.logical_and(xi == xl, strip == 0), jnp.logical_and(xi == 2 * xl, strip == strips - 1)
    )
    edge_y = yi == 0

    def edge_z(z, width):
        return jnp.logical_or(
            jnp.logical_and(z == width, slab == 0),
            jnp.logical_and(z == 2 * width, slab == slabs - 1),
        )

    table = table_ref[...]
    for block in range(9):
        z_at, x_at = place(block // 3, slab), place(block % 3, strip)

        def soil_step(i, carry, block=block, z_at=z_at, x_at=x_at):
            z = z_at * zl + i
            soil = state_refs[block][zl + i].astype(jnp.int32)
            p = head_refs[block][i]
            forcing = state_refs[block % 3][2 * zl]
            dtheta, alpha, shape_n, k_sat, expon_m = (look_up(table, k, soil) for k in range(5))
            layer = (slab * zl - zl + z).astype(jnp.float32)
            depth = jnp.full((1, ny), layer, jnp.float32)
            sink = forcing * jnp.exp(-ROOT_DECAY * depth / (slabs * zl))
            log_s = jnp.log(jnp.abs(alpha * p))
            log_p = shape_n * log_s
            log_b = jnp.log(1.0 + jnp.exp(log_p))
            root = jnp.exp(-0.5 * expon_m * log_b)
            sat = root * root
            slope = expon_m * shape_n * alpha * sat * jnp.exp((shape_n - 1.0) * log_s - log_b)
            cond[z, x_at] = k_sat * root * jnp.square(1.0 - jnp.exp(expon_m * (log_p - log_b)))
            stor[z, x_at] = slope * (dtheta / DT + sink)
            g = sink * sat
            if first:
                sat_out[z, x_at] = sat
            else:
                g = g + dtheta * (sat - sat_old_ref[z, x_at]) / DT
            grow[z, x_at] = g
            head[z, x_at] = p
            return carry

        skip = 0 if block < 3 else 1
        start = jnp.where(z_at == 0, skip, 0)
        lax.fori_loop(0, zl - skip, lambda i, c: soil_step(start + i, c), 0, unroll=zl - skip)

    def face_z(z):
        both = 0.5 * (slab_of(cond, z - 1) + slab_of(cond, z))
        return both * jnp.where(edge_z(z, zl), 0.0, 1.0)

    fz[2] = face_z(2)

    def face_step(z, carry):
        c, p = slab_of(cond, z), slab_of(head, z)
        across = jnp.where(edge_x, 0.0, 0.5 * (c + roll(c, 1, 0)))
        along = jnp.where(edge_y, 0.0, 0.5 * (c + roll(c, 1, 1)))
        low, high = fz[z], face_z(z + 1)
        flux_x = across * (roll(p, 1, 0) - p)
        flux_y = along * (roll(p, 1, 1) - p)
        p_low = slab_of(head, z - 1)
        p_high = slab_of(head, z + 1)
        flux_low = low * (p_low - p + GRAVITY)
        flux_high = high * (p - p_high + GRAVITY)
        source = (flux_x - roll(flux_x, -1, 0)) + (flux_y - roll(flux_y, -1, 1))
        source = source + (flux_low - flux_high) - slab_of(grow, z)
        diagonal = slab_of(stor, z) + (across + roll(across, -1, 0)) + (along + roll(along, -1, 1))
        inverse = 1.0 / (diagonal + (low + high))
        fx[z], fy[z], fz[z + 1] = across, along, high
        src[z], inv[z] = source, inverse
        err[z] = jnp.where(parity0 == (z & 1), source * inverse, 0.0)
        return carry

    lax.fori_loop(2, zw - 2, face_step, 0, unroll=4)

    def sum0(z):
        return neighbour_sum(
            err[z],
            err[z - 1],
            err[z + 1],
            fx[z],
            fy[z],
            fz[z],
            fz[z + 1],
            1,
        )

    def smooth_step(z, carry):
        updated = (src[z] + sum0(z)) * inv[z]
        err[z] = jnp.where(parity0 == (z & 1), err[z], updated)
        return carry

    lax.fori_loop(3, zw - 3, smooth_step, 0, unroll=3)

    def coarse_step(k, carry):
        za, zb = 2 * k, 2 * k + 1
        resid = jnp.where(parity0 == 0, sum0(za), sum0(zb))
        src1[k] = spread_pairs(spread_pairs(resid, x_low, 1, 0), y_low, 1, 1)
        stor1[k] = spread_pairs(
            spread_pairs(slab_of(stor, za) + slab_of(stor, zb), x_low, 1, 0), y_low, 1, 1
        )
        across = spread_pairs(fx[za] + fx[zb], y_low, 1, 1)
        fx1[k] = jnp.where(x_low, across, roll(across, 1, 0))
        along = spread_pairs(fy[za] + fy[zb], x_low, 1, 0)
        fy1[k] = jnp.where(y_low, along, roll(along, 1, 1))
        fz1[k] = spread_pairs(spread_pairs(fz[za], x_low, 1, 0), y_low, 1, 1)
        return carry

    lax.fori_loop(2, zw // 2 - 1, coarse_step, 0, unroll=3)

    def first1(k, carry):
        across, along = fx1[k], fy1[k]
        diagonal = stor1[k] + (across + roll(across, -2, 0)) + (along + roll(along, -2, 1))
        inverse = 1.0 / (diagonal + (fz1[k] + fz1[k + 1]))
        inv1[k] = inverse
        err1[k] = jnp.where(parity1 == (k & 1), src1[k] * inverse, 0.0)
        return carry

    low1, high1 = zl // 2 - 2, zl + 2
    lax.fori_loop(low1, high1, first1, 0, unroll=4)

    def sum1(k):
        return neighbour_sum(
            err1[k], err1[k - 1], err1[k + 1], fx1[k], fy1[k], fz1[k], fz1[k + 1], 2
        )

    def second1(k, carry):
        updated = (src1[k] + sum1(k)) * inv1[k]
        err1[k] = jnp.where(parity1 == (k & 1), err1[k], updated)
        return carry

    lax.fori_loop(low1 + 1, high1 - 1, second1, 0, unroll=3)

    rows2[...] = jnp.zeros(rows2.shape, jnp.float32)
    own1 = zl // 2
    for k2 in range(zl // 4):
        ka, kb = own1 + 2 * k2, own1 + 2 * k2 + 1
        resid = jnp.where(parity1 == 0, sum1(ka), sum1(kb))
        terms = (
            spread_pairs(spread_pairs(resid, x_low2, 2, 0), y_low2, 2, 1),
            spread_pairs(spread_pairs(stor1[ka] + stor1[kb], x_low2, 2, 0), y_low2, 2, 1),
            spread_pairs(fx1[ka] + fx1[kb], y_low2, 2, 1),
            spread_pairs(fy1[ka] + fy1[kb], x_low2, 2, 0),
            spread_pairs(spread_pairs(fz1[ka], x_low2, 2, 0), y_low2, 2, 1),
        )
        for t, term in enumerate(terms):
            for x2 in range(xl // 4):
                at = (t * (xl // 4) + x2) * (zl // 4) + k2
                x = xl + 4 * x2
                rows2[at : at + 1, :] = term[x : x + 1, :]
    pick_shape = (ny, ny // 4)
    pick = lax.broadcasted_iota(jnp.int32, pick_shape, 0) == 4 * lax.broadcasted_iota(
        jnp.int32, pick_shape, 1
    )
    payload_ref[0 : rows2.shape[0], :] = jnp.dot(
        rows2[...], jnp.where(pick, 1.0, 0.0), precision=HI, preferred_element_type=jnp.float32
    )
    own = slice(xl, 2 * xl)
    here = [err1[own1 + k][own] for k in range(4)]
    xo, yo = x_low[own], y_low[own]
    plane = jnp.where(xo, jnp.where(yo, here[0], here[1]), jnp.where(yo, here[2], here[3]))
    base = rows2.shape[0]
    for c in range(ny // 128):
        payload_ref[base + 8 * c : base + 8 * c + 8, :] = plane[:, 128 * c : 128 * c + 128]


def solve_blocks(block, factors, answer, strips, slabs):
    zero = jnp.zeros((1, 128), jnp.float32)

    def entry(kind, b, z):
        return block[kind, b, 2 * z : 2 * z + 1, :]

    pairs = [(i, j) for i in range(slabs) for j in range(i, slabs)]

    def forward(b, carry):
        a = dict(zip(pairs, carry[: len(pairs)]))
        r = list(carry[len(pairs) :]) + [zero] * slabs
        for z in range(slabs):
            here, after = entry(2, b, z), entry(2, b + 1, z)
            low = entry(3, b, z)
            high = entry(3, b, z + 1) if z + 1 < slabs else zero
            a[z, z] = a[z, z] + (entry(1, b, z) + here + after + low + high)
            if z + 1 < slabs:
                a[z, z + 1] = a[z, z + 1] - high
            a[z, slabs + z] = -after
            r[z] = r[z] + entry(0, b, z)
        for i in range(slabs):
            inverse = 1.0 / a[i, i]
            others = list(range(i + 1, slabs + i + 1))
            scaled = [a[i, j] * inverse if (i, j) in a else None for j in others]
            for n, j in enumerate(others):
                if scaled[n] is None:
                    continue
                for k in others[n:]:
                    if (i, k) in a:
                        a[j, k] = a.get((j, k), zero) - scaled[n] * a[i, k]
                r[j] = r[j] - scaled[n] * r[i]
                factors[b, i * (slabs + 1) + n] = scaled[n]
            factors[b, i * (slabs + 1) + slabs] = r[i] * inverse
        nexts = [a.get((slabs + i, slabs + j), zero) for i, j in pairs]
        return tuple(nexts + r[slabs:])

    unroll = strips if strips <= 8 else 1
    lax.fori_loop(0, strips, forward, (zero,) * (len(pairs) + slabs), unroll=unroll)

    def backward(n, above):
        b = strips - 1 - n
        x = [None] * slabs + list(above)
        for i in reversed(range(slabs)):
            value = factors[b, i * (slabs + 1) + slabs]
            for n, j in enumerate(range(i + 1, slabs + i + 1)):
                value = value - factors[b, i * (slabs + 1) + n] * x[j]
            x[i] = value
            answer[b, 2 * i : 2 * i + 2, :] = jnp.broadcast_to(value, (2, 128))
        return tuple(x[:slabs])

    lax.fori_loop(0, strips, backward, (zero,) * slabs, unroll=unroll)


def up_kernel(slabs, strips, zl, xl, counts, *refs):
    where_ref, refs = refs[0], refs[1:]
    pieces, refs = refs[: len(counts)], refs[len(counts) :]
    near, refs = refs[:3], refs[3:]
    e0_in, src0, inv0, fx0, fy0, fz0 = refs[:6]
    src1, inv1, fx1, fy1, fz1 = refs[6:11]
    head_ref, out_ref = refs[11], refs[12]
    a2, block, factors, answer, e2, picked, wide, e1, e0 = refs[13:]
    strip, slab = where_ref[0], where_ref[1]
    x2, z2 = xl // 4, zl // 4
    rows2 = strips * x2
    ny = head_ref.shape[2]

    index = 0
    for ref, count in zip(pieces, counts):
        for j in range(count):
            at = jnp.bitwise_xor(strip, index)
            for g in range(slabs):
                piece = ref[j, jnp.bitwise_xor(slab, g)]
                for t in range(5):
                    for x in range(x2):
                        k = (t * x2 + x) * z2
                        a2[t, at * x2 + x, g * z2 : g * z2 + z2, :] = piece[k : k + z2, :]
            index += 1

    shape = (rows2, 8, 128)
    source, store, fx, fy, fz = (a2[t] for t in range(5))

    def shift_x(v, step):
        if step > 0:
            return jnp.concatenate([jnp.zeros_like(v[:1]), v[:-1]], axis=0)
        return jnp.concatenate([v[1:], jnp.zeros_like(v[:1])], axis=0)

    def along(v, step, axis):
        return pltpu.roll(v, step % v.shape[axis], axis)

    fx_up, fy_up, fz_up = shift_x(fx, -1), along(fy, -1, 2), along(fz, -1, 1)
    inverse = 1.0 / (store + (fx + fx_up) + (fy + fy_up) + (fz + fz_up))
    parity = (
        lax.broadcasted_iota(jnp.int32, shape, 0)
        + lax.broadcasted_iota(jnp.int32, shape, 1)
        + lax.broadcasted_iota(jnp.int32, shape, 2)
    ) & 1
    even = parity == 0

    def sum2(e):
        total = fx * shift_x(e, 1) + fx_up * shift_x(e, -1)
        total = total + (fy * along(e, 1, 2) + fy_up * along(e, -1, 2))
        return total + (fz * along(e, 1, 1) + fz_up * along(e, -1, 1))

    e = jnp.where(even, source * inverse, 0.0)
    e = jnp.where(even, e, (source + sum2(e)) * inverse)
    resid = jnp.where(even, sum2(e), 0.0)

    def blocks(v, both_rows, both_layers):
        v = v.reshape(strips, x2, 8, 128)
        v = v[:, 0] + v[:, 1] if both_rows else v[:, 0]
        v = jnp.sum(v, axis=2, keepdims=True)
        v = jnp.broadcast_to(v, (strips, 8, 128))
        return v + along(v, -1, 1) if both_layers else v

    block[0, 0:strips] = blocks(resid, True, True)
    block[1, 0:strips] = blocks(store, True, True)
    block[2, 0:strips] = blocks(fx, False, True)
    block[2, strips] = jnp.zeros((8, 128), jnp.float32)
    block[3, 0:strips] = blocks(fz, True, False)
    solve_blocks(block, factors, answer, strips, slabs)
    add = jnp.broadcast_to(answer[...][:, None], (strips, x2, 8, 128)).reshape(shape)
    e = e + add
    e = jnp.where(even, (source + sum2(e)) * inverse, e)
    e = jnp.where(even, e, (source + sum2(e)) * inverse)
    e2[...] = jnp.zeros(e2.shape, jnp.float32)
    e2[x2 : x2 + rows2, 8:16, :] = e

    picked[...] = jnp.zeros(picked.shape, jnp.float32)
    for z in range(3 * z2):
        for x in range(3 * x2):
            at = z * 3 * x2 + x
            picked[at : at + 1, :] = e2[
                strip * x2 + x, pl.ds(8 - z2 + slab * z2 + z, 1), :
            ]
    spread_shape = (ny // 4, ny)
    spread = lax.broadcasted_iota(jnp.int32, spread_shape, 0) == (
        lax.broadcasted_iota(jnp.int32, spread_shape, 1) >> 2
    )
    wide[...] = jnp.dot(
        picked[...], jnp.where(spread, 1.0, 0.0), precision=HI, preferred_element_type=jnp.float32
    )

    zl1 = zl // 2
    small = (xl, ny)
    xo = (lax.broadcasted_iota(jnp.int32, small, 0) & 1) == 0
    yo = (lax.broadcasted_iota(jnp.int32, small, 1) & 1) == 0
    for zb in range(3):
        g = slab + (zb - 1)
        inside = jnp.logical_and(g >= 0, g < slabs)
        m = jnp.bitwise_xor(slab, jnp.clip(g, 0, slabs - 1))
        keep = jnp.where(inside, 1.0, 0.0)
        for which in range(3):
            xb = place(which, strip)
            tile = near[which][m]
            plane = jnp.concatenate(
                [tile[8 * c : 8 * c + 8, :] for c in range(ny // 128)], axis=1
            )
            plane = plane * keep
            for k in range(4):
                xk, yk = k // 2, k % 2
                v = jnp.where(jnp.logical_and(xo == (xk == 0), yo == (yk == 0)), plane, 0.0)
                v = v + roll(v, 1 if xk == 0 else -1, 0)
                v = v + roll(v, 1 if yk == 0 else -1, 1)
                e1[zb * zl1 + k, xb] = v
    window = (3 * xl, ny)
    for k in range(3 * zl1):
        rows = [wide[k // 2 * 3 * x2 + x : k // 2 * 3 * x2 + x + 1, :] for x in range(3 * x2)]
        rows = [jnp.broadcast_to(row, (4, ny)) for row in rows]
        rows = [jnp.concatenate(rows[x2 * b : x2 * b + x2], axis=0)[None] for b in range(3)]
        e1[k] = e1[k] + jnp.concatenate(rows, axis=0)

    def at1(k):
        return e1[k].reshape(window)

    xi = lax.broadcasted_iota(jnp.int32, window, 0)
    yi = lax.broadcasted_iota(jnp.int32, window, 1)
    parity0 = (xi + yi) & 1
    parity1 = ((xi >> 1) + (yi >> 1)) & 1

    def level1(k, colour):
        total = neighbour_sum(
            at1(k), at1(k - 1), at1(k + 1), fx1[k], fy1[k], fz1[k], fz1[k + 1], 2
        )
        updated = (src1[k] + total) * inv1[k]
        e1[k] = jnp.where(parity1 == ((k + colour) & 1), updated, at1(k)).reshape(3, xl, ny)

    def up1(colour, reach):
        def step(k, carry):
            level1(k, colour)
            return carry

        lax.fori_loop(zl1 - reach, 2 * zl1 + reach, step, 0, unroll=2)

    up1(0, 2)
    up1(1, 1)

    def join(i, carry):
        e0[i] = e0_in[i + zl - 2] + at1((zl - 2 + i) // 2)
        return carry

    lax.fori_loop(0, zl + 4, join, 0, unroll=3)

    def up0(colour, reach):
        def step(i, carry):
            z = i + zl - 2
            total = neighbour_sum(
                e0[i], e0[i - 1], e0[i + 1], fx0[z], fy0[z], fz0[z], fz0[z + 1], 1
            )
            updated = (src0[z] + total) * inv0[z]
            e0[i] = jnp.where(parity0 == ((i + colour) & 1), updated, e0[i])
            return carry

        lax.fori_loop(2 - reach, zl + 2 + reach, step, 0, unroll=2)

    up0(0, 1)
    up0(1, 0)
    for z in range(zl):
        out_ref[z] = head_ref[z] + e0[z + 2][xl : 2 * xl]


VMEM = pl.BlockSpec(memory_space=pltpu.VMEM)
SMEM = pl.BlockSpec(memory_space=pltpu.SMEM)


def f32(*shape):
    return jax.ShapeDtypeStruct(shape, jnp.float32)


def down(first, slabs, strips, zl, xl, ny, where, table, state, head=None, sat_old=None):
    zw, xw = 3 * zl, 3 * xl
    rows2 = 5 * (xl // 4) * (zl // 4)
    rows2 = -(-rows2 // 8) * 8
    out_shape = [f32(rows2 + 8 * ny // 128, 128)]
    out_shape += [f32(zw, xw, ny)] * 6 + [f32(zw // 2, xw, ny)] * 5
    operands = [where, table, *state]
    if first:
        out_shape.append(f32(zw, 3, xl, ny))
    else:
        operands += [*head, sat_old]
    split = pltpu.VMEM((zw, 3, xl, ny), jnp.float32)
    half = pltpu.VMEM((zw // 2, xw, ny), jnp.float32)
    return pl.pallas_call(
        functools.partial(down_kernel, first, slabs, strips, zl, xl),
        out_shape=out_shape,
        in_specs=[SMEM] + [VMEM] * (len(operands) - 1),
        out_specs=[VMEM] * len(out_shape),
        scratch_shapes=[split] * 4 + [half] * 2 + [pltpu.VMEM((rows2, ny), jnp.float32)],
        compiler_params=pltpu.CompilerParams(vmem_limit_bytes=30 * 1024 * 1024),
    )(*operands)


def up(slabs, strips, zl, xl, ny, where, pieces, near, kept, head):
    x2, z2 = xl // 4, zl // 4
    counts = [p.shape[0] for p in pieces]
    operands = [where, *pieces, *near, *kept, head]
    n = -(-9 * x2 * z2 // 8) * 8
    scratch = [
        pltpu.VMEM((5, strips * x2, 8, 128), jnp.float32),
        pltpu.VMEM((4, strips + 1, 8, 128), jnp.float32),
        pltpu.VMEM((strips, slabs * (slabs + 1), 1, 128), jnp.float32),
        pltpu.VMEM((strips, 8, 128), jnp.float32),
        pltpu.VMEM(((strips + 2) * x2, 24, 128), jnp.float32),
        pltpu.VMEM((n, ny // 4), jnp.float32),
        pltpu.VMEM((n, ny), jnp.float32),
        pltpu.VMEM((3 * zl // 2, 3, xl, ny), jnp.float32),
        pltpu.VMEM((zl + 4, 3 * xl, ny), jnp.float32),
    ]
    return pl.pallas_call(
        functools.partial(up_kernel, slabs, strips, zl, xl, counts),
        out_shape=f32(zl, xl, ny),
        in_specs=[SMEM] + [VMEM] * (len(operands) - 1),
        out_specs=VMEM,
        scratch_shapes=scratch,
        compiler_params=pltpu.CompilerParams(vmem_limit_bytes=30 * 1024 * 1024),
    )(*operands)


def swapped(x, axis, mask):
    return lax.ppermute(x, axis, [(i, i ^ mask) for i in range(lax.axis_size(axis))])


def crossed(x, strip_mask, slab_mask):
    strips, slabs = lax.axis_size("xy"), lax.axis_size("gz")
    pairs = [
        (i * slabs + j, (i ^ strip_mask) * slabs + (j ^ slab_mask))
        for i in range(strips)
        for j in range(slabs)
    ]
    return lax.ppermute(x, ("xy", "gz"), pairs)


def odd_pairs(x, axis):
    size = lax.axis_size(axis)
    pairs = [(i, i + 1) for i in range(1, size - 1, 2)]
    return lax.ppermute(x, axis, pairs + [(j, i) for i, j in pairs])


def neighbourhood(x):
    row = [x, swapped(x, "xy", 1), odd_pairs(x, "xy")]
    return row + [swapped(v, "gz", 1) for v in row] + [odd_pairs(v, "gz") for v in row]


def gather_strips(own, partner):
    size = lax.axis_size("xy")
    x = jnp.stack([own, partner])
    if size == 8:
        return [x] + [swapped(x, "xy", m) for m in (2, 4, 6)]
    mask = 2
    while mask < size:
        x = jnp.concatenate([x, swapped(x, "xy", mask)])
        mask *= 2
    return [x]


def per_device(head_old, soil_type, soil_table, land_mask, sun_bin):
    zl, xl, ny = head_old.shape
    strips, slabs = lax.axis_size("xy"), lax.axis_size("gz")
    where = jnp.stack([lax.axis_index("xy"), lax.axis_index("gz")]).astype(jnp.int32)
    resid, sat, alpha, shape_n, k_sat = soil_table
    table = jnp.stack([sat - resid, alpha, shape_n, k_sat, 1.0 - 1.0 / shape_n])
    table = jnp.pad(table, ((0, 3), (0, 128 - table.shape[1])))
    sun_share = jnp.maximum(0.0, jnp.sin(math.pi * (sun_bin.astype(jnp.float32) - 6.0) / 12.0))
    forcing = ET_PEAK * sun_share * land_mask.astype(jnp.float32)
    across = ((0, 0), (0, 0))
    soil = jnp.pad(soil_type, ((zl, 1), *across)).astype(jnp.float32)
    own = jnp.pad(head_old, ((0, zl + 1), *across)) + soil
    own = own + jnp.pad(forcing[None], ((2 * zl, 0), *across))
    state = neighbourhood(own)
    sizes = (slabs, strips, zl, xl, ny)
    base = -(-5 * (xl // 4) * (zl // 4) // 8) * 8

    def finish(payload, kept, head):
        pair = [payload, swapped(payload, "gz", 1)]
        pair = jnp.stack(pair)
        far = [crossed(pair, i, j) for i, j in ((0, 2), (1, 0), (1, 2))]
        full = jnp.concatenate([pair, far[0]])
        partner = jnp.concatenate([far[1], far[2]])
        pieces = gather_strips(full[:, :base], partner[:, :base])
        near = [full[:, base:], partner[:, base:], odd_pairs(full[:, base:], "xy")]
        return up(*sizes, where, pieces, near, kept, head)

    payload, *kept, sat_old = down(True, *sizes, where, table, state)
    head = finish(payload, kept, head_old)
    payload, *kept = down(
        False, *sizes, where, table, state, neighbourhood(head), sat_old
    )
    return finish(payload, kept, head)


def solution(mesh):
    in_specs = (P("gz", "xy", None), P("gz", "xy", None), P(), P("xy", None), P("xy", None))
    out_specs = P("gz", "xy", None)
    return jax.shard_map(
        per_device, mesh=mesh, in_specs=in_specs, out_specs=out_specs, check_vma=False
    )
```

```python
import functools
import math

import jax
import jax.numpy as jnp
from jax import lax
from jax.experimental import pallas as pl
from jax.experimental.pallas import tpu as pltpu
from jax.sharding import PartitionSpec as P

DT = 20.0
ET_PEAK = 0.008
GRAVITY = 0.1
ROOT_DECAY = 3.0
HI = lax.Precision.HIGHEST


def roll(value, shift, axis):
    return pltpu.roll(value, shift % value.shape[axis], axis)


def place(which, index):
    if which == 0:
        return 1
    odd = index & 1
    return 2 - 2 * odd if which == 1 else 2 * odd


def spread_pairs(value, low, step, axis):
    return value + jnp.where(low, roll(value, -step, axis), roll(value, step, axis))


def neighbour_sum(e, below, above, fx, fy, fz, fz_up, step):
    total = fx * roll(e, step, 0) + roll(fx * e, -step, 0)
    total = total + (fy * roll(e, step, 1) + roll(fy * e, -step, 1))
    return total + (fz * below + fz_up * above)


def look_up(table, row, index):
    picked = jnp.broadcast_to(table[row : row + 1, :], (8, 128))
    rows = []
    for r in range(0, index.shape[0], 8):
        cols = []
        for c in range(0, index.shape[1], 128):
            at = index[r : r + 8, c : c + 128]
            cols.append(jnp.take_along_axis(picked, at, axis=1, mode="promise_in_bounds"))
        rows.append(jnp.concatenate(cols, axis=1))
    return jnp.concatenate(rows, axis=0)


def down_kernel(first, slabs, strips, zl, xl, *refs):
    where_ref, table_ref = refs[0], refs[1]
    refs = refs[2:]
    state_refs, refs = refs[:9], refs[9:]
    if first:
        head_refs = state_refs
    else:
        head_refs, refs = refs[:9], refs[9:]
        sat_old_ref, refs = refs[0], refs[1:]
    payload_ref, refs = refs[0], refs[1:]
    err, src, inv, fx, fy, fz = refs[:6]
    src1, inv1, fx1, fy1, fz1 = refs[6:11]
    refs = refs[11:]
    if first:
        sat_out, refs = refs[0], refs[1:]
    head, cond, stor, grow, stor1, err1, rows2 = refs

    strip, slab = where_ref[0], where_ref[1]
    zw, xw = 3 * zl, 3 * xl
    ny = head.shape[3]
    shape = (xw, ny)

    def slab_of(ref, z):
        return ref[z].reshape(shape)

    xi = lax.broadcasted_iota(jnp.int32, shape, 0)
    yi = lax.broadcasted_iota(jnp.int32, shape, 1)
    parity0 = (xi + yi) & 1
    parity1 = ((xi >> 1) + (yi >> 1)) & 1
    x_low, y_low = (xi & 1) == 0, (yi & 1) == 0
    x_low2, y_low2 = (xi & 2) == 0, (yi & 2) == 0
    edge_x = jnp.logical_or(
        jnp.logical_and(xi == xl, strip == 0), jnp.logical_and(xi == 2 * xl, strip == strips - 1)
    )
    edge_y = yi == 0

    def edge_z(z, width):
        return jnp.logical_or(
            jnp.logical_and(z == width, slab == 0),
            jnp.logical_and(z == 2 * width, slab == slabs - 1),
        )

    table = table_ref[...]
    for block in range(9):
        z_at, x_at = place(block // 3, slab), place(block % 3, strip)

        def soil_step(i, carry, block=block, z_at=z_at, x_at=x_at):
            z = z_at * zl + i
            soil = state_refs[block][zl + i].astype(jnp.int32)
            p = head_refs[block][i]
            forcing = state_refs[block % 3][2 * zl]
            dtheta, alpha, shape_n, k_sat, expon_m = (look_up(table, k, soil) for k in range(5))
            layer = (slab * zl - zl + z).astype(jnp.float32)
            depth = jnp.full((1, ny), layer, jnp.float32)
            sink = forcing * jnp.exp(-ROOT_DECAY * depth / (slabs * zl))
            log_s = jnp.log(jnp.abs(alpha * p))
            log_p = shape_n * log_s
            log_b = jnp.log(1.0 + jnp.exp(log_p))
            root = jnp.exp(-0.5 * expon_m * log_b)
            sat = root * root
            slope = expon_m * shape_n * alpha * sat * jnp.exp((shape_n - 1.0) * log_s - log_b)
            cond[z, x_at] = k_sat * root * jnp.square(1.0 - jnp.exp(expon_m * (log_p - log_b)))
            stor[z, x_at] = slope * (dtheta / DT + sink)
            g = sink * sat
            if first:
                sat_out[z, x_at] = sat
            else:
                g = g + dtheta * (sat - sat_old_ref[z, x_at]) / DT
            grow[z, x_at] = g
            head[z, x_at] = p
            return carry

        skip = 0 if block < 3 else 1
        start = jnp.where(z_at == 0, skip, 0)
        lax.fori_loop(0, zl - skip, lambda i, c: soil_step(start + i, c), 0, unroll=zl - skip)

    def face_z(z):
        both = 0.5 * (slab_of(cond, z - 1) + slab_of(cond, z))
        return both * jnp.where(edge_z(z, zl), 0.0, 1.0)

    fz[2] = face_z(2)

    def face_step(z, carry):
        c, p = slab_of(cond, z), slab_of(head, z)
        across = jnp.where(edge_x, 0.0, 0.5 * (c + roll(c, 1, 0)))
        along = jnp.where(edge_y, 0.0, 0.5 * (c + roll(c, 1, 1)))
        low, high = fz[z], face_z(z + 1)
        flux_x = across * (roll(p, 1, 0) - p)
        flux_y = along * (roll(p, 1, 1) - p)
        p_low = slab_of(head, z - 1)
        p_high = slab_of(head, z + 1)
        flux_low = low * (p_low - p + GRAVITY)
        flux_high = high * (p - p_high + GRAVITY)
        source = (flux_x - roll(flux_x, -1, 0)) + (flux_y - roll(flux_y, -1, 1))
        source = source + (flux_low - flux_high) - slab_of(grow, z)
        diagonal = slab_of(stor, z) + (across + roll(across, -1, 0)) + (along + roll(along, -1, 1))
        inverse = 1.0 / (diagonal + (low + high))
        fx[z], fy[z], fz[z + 1] = across, along, high
        src[z], inv[z] = source, inverse
        err[z] = jnp.where(parity0 == (z & 1), source * inverse, 0.0)
        return carry

    lax.fori_loop(2, zw - 2, face_step, 0, unroll=5)

    def sum0(z):
        return neighbour_sum(
            err[z],
            err[z - 1],
            err[z + 1],
            fx[z],
            fy[z],
            fz[z],
            fz[z + 1],
            1,
        )

    def smooth_step(z, carry):
        updated = (src[z] + sum0(z)) * inv[z]
        err[z] = jnp.where(parity0 == (z & 1), err[z], updated)
        return carry

    lax.fori_loop(3, zw - 3, smooth_step, 0, unroll=6)

    def coarse_step(k, carry):
        za, zb = 2 * k, 2 * k + 1
        resid = jnp.where(parity0 == 0, sum0(za), sum0(zb))
        src1[k] = spread_pairs(spread_pairs(resid, x_low, 1, 0), y_low, 1, 1)
        stor1[k] = spread_pairs(
            spread_pairs(slab_of(stor, za) + slab_of(stor, zb), x_low, 1, 0), y_low, 1, 1
        )
        across = spread_pairs(fx[za] + fx[zb], y_low, 1, 1)
        fx1[k] = jnp.where(x_low, across, roll(across, 1, 0))
        along = spread_pairs(fy[za] + fy[zb], x_low, 1, 0)
        fy1[k] = jnp.where(y_low, along, roll(along, 1, 1))
        fz1[k] = spread_pairs(spread_pairs(fz[za], x_low, 1, 0), y_low, 1, 1)
        return carry

    lax.fori_loop(2, zw // 2 - 1, coarse_step, 0, unroll=3)

    def first1(k, carry):
        across, along = fx1[k], fy1[k]
        diagonal = stor1[k] + (across + roll(across, -2, 0)) + (along + roll(along, -2, 1))
        inverse = 1.0 / (diagonal + (fz1[k] + fz1[k + 1]))
        inv1[k] = inverse
        err1[k] = jnp.where(parity1 == (k & 1), src1[k] * inverse, 0.0)
        return carry

    low1, high1 = zl // 2 - 2, zl + 2
    lax.fori_loop(low1, high1, first1, 0, unroll=4)

    def sum1(k):
        return neighbour_sum(
            err1[k], err1[k - 1], err1[k + 1], fx1[k], fy1[k], fz1[k], fz1[k + 1], 2
        )

    def second1(k, carry):
        updated = (src1[k] + sum1(k)) * inv1[k]
        err1[k] = jnp.where(parity1 == (k & 1), err1[k], updated)
        return carry

    lax.fori_loop(low1 + 1, high1 - 1, second1, 0, unroll=3)

    rows2[...] = jnp.zeros(rows2.shape, jnp.float32)
    own1 = zl // 2
    for k2 in range(zl // 4):
        ka, kb = own1 + 2 * k2, own1 + 2 * k2 + 1
        resid = jnp.where(parity1 == 0, sum1(ka), sum1(kb))
        terms = (
            spread_pairs(spread_pairs(resid, x_low2, 2, 0), y_low2, 2, 1),
            spread_pairs(spread_pairs(stor1[ka] + stor1[kb], x_low2, 2, 0), y_low2, 2, 1),
            spread_pairs(fx1[ka] + fx1[kb], y_low2, 2, 1),
            spread_pairs(fy1[ka] + fy1[kb], x_low2, 2, 0),
            spread_pairs(spread_pairs(fz1[ka], x_low2, 2, 0), y_low2, 2, 1),
        )
        for t, term in enumerate(terms):
            for x2 in range(xl // 4):
                at = (t * (xl // 4) + x2) * (zl // 4) + k2
                x = xl + 4 * x2
                rows2[at : at + 1, :] = term[x : x + 1, :]
    pick_shape = (ny, ny // 4)
    pick = lax.broadcasted_iota(jnp.int32, pick_shape, 0) == 4 * lax.broadcasted_iota(
        jnp.int32, pick_shape, 1
    )
    payload_ref[0 : rows2.shape[0], :] = jnp.dot(
        rows2[...], jnp.where(pick, 1.0, 0.0), precision=HI, preferred_element_type=jnp.float32
    )
    own = slice(xl, 2 * xl)
    here = [err1[own1 + k][own] for k in range(4)]
    xo, yo = x_low[own], y_low[own]
    plane = jnp.where(xo, jnp.where(yo, here[0], here[1]), jnp.where(yo, here[2], here[3]))
    base = rows2.shape[0]
    for c in range(ny // 128):
        payload_ref[base + 8 * c : base + 8 * c + 8, :] = plane[:, 128 * c : 128 * c + 128]


def solve_blocks(block, factors, answer, strips, slabs):
    zero = jnp.zeros((1, 128), jnp.float32)

    def entry(kind, b, z):
        return block[kind, b, 2 * z : 2 * z + 1, :]

    pairs = [(i, j) for i in range(slabs) for j in range(i, slabs)]

    def forward(b, carry):
        a = dict(zip(pairs, carry[: len(pairs)]))
        r = list(carry[len(pairs) :]) + [zero] * slabs
        for z in range(slabs):
            here, after = entry(2, b, z), entry(2, b + 1, z)
            low = entry(3, b, z)
            high = entry(3, b, z + 1) if z + 1 < slabs else zero
            a[z, z] = a[z, z] + (entry(1, b, z) + here + after + low + high)
            if z + 1 < slabs:
                a[z, z + 1] = a[z, z + 1] - high
            a[z, slabs + z] = -after
            r[z] = r[z] + entry(0, b, z)
        for i in range(slabs):
            inverse = 1.0 / a[i, i]
            others = list(range(i + 1, slabs + i + 1))
            scaled = [a[i, j] * inverse if (i, j) in a else None for j in others]
            for n, j in enumerate(others):
                if scaled[n] is None:
                    continue
                for k in others[n:]:
                    if (i, k) in a:
                        a[j, k] = a.get((j, k), zero) - scaled[n] * a[i, k]
                r[j] = r[j] - scaled[n] * r[i]
                factors[b, i * (slabs + 1) + n] = scaled[n]
            factors[b, i * (slabs + 1) + slabs] = r[i] * inverse
        nexts = [a.get((slabs + i, slabs + j), zero) for i, j in pairs]
        return tuple(nexts + r[slabs:])

    unroll = strips if strips <= 8 else 1
    lax.fori_loop(0, strips, forward, (zero,) * (len(pairs) + slabs), unroll=unroll)

    def backward(n, above):
        b = strips - 1 - n
        x = [None] * slabs + list(above)
        for i in reversed(range(slabs)):
            value = factors[b, i * (slabs + 1) + slabs]
            for n, j in enumerate(range(i + 1, slabs + i + 1)):
                value = value - factors[b, i * (slabs + 1) + n] * x[j]
            x[i] = value
            answer[b, 2 * i : 2 * i + 2, :] = jnp.broadcast_to(value, (2, 128))
        return tuple(x[:slabs])

    lax.fori_loop(0, strips, backward, (zero,) * slabs, unroll=unroll)


def up_kernel(slabs, strips, zl, xl, counts, *refs):
    where_ref, refs = refs[0], refs[1:]
    pieces, refs = refs[: len(counts)], refs[len(counts) :]
    near, refs = refs[:3], refs[3:]
    e0_in, src0, inv0, fx0, fy0, fz0 = refs[:6]
    src1, inv1, fx1, fy1, fz1 = refs[6:11]
    head_ref, out_ref = refs[11], refs[12]
    a2, block, factors, answer, e2, picked, wide, e1, e0 = refs[13:]
    strip, slab = where_ref[0], where_ref[1]
    x2, z2 = xl // 4, zl // 4
    rows2 = strips * x2
    ny = head_ref.shape[2]

    index = 0
    for ref, count in zip(pieces, counts):
        for j in range(count):
            at = jnp.bitwise_xor(strip, index)
            for g in range(slabs):
                piece = ref[j, jnp.bitwise_xor(slab, g)]
                for t in range(5):
                    for x in range(x2):
                        k = (t * x2 + x) * z2
                        a2[t, at * x2 + x, g * z2 : g * z2 + z2, :] = piece[k : k + z2, :]
            index += 1

    shape = (rows2, 8, 128)
    source, store, fx, fy, fz = (a2[t] for t in range(5))

    def shift_x(v, step):
        if step > 0:
            return jnp.concatenate([jnp.zeros_like(v[:1]), v[:-1]], axis=0)
        return jnp.concatenate([v[1:], jnp.zeros_like(v[:1])], axis=0)

    def along(v, step, axis):
        return pltpu.roll(v, step % v.shape[axis], axis)

    fx_up, fy_up, fz_up = shift_x(fx, -1), along(fy, -1, 2), along(fz, -1, 1)
    inverse = 1.0 / (store + (fx + fx_up) + (fy + fy_up) + (fz + fz_up))
    parity = (
        lax.broadcasted_iota(jnp.int32, shape, 0)
        + lax.broadcasted_iota(jnp.int32, shape, 1)
        + lax.broadcasted_iota(jnp.int32, shape, 2)
    ) & 1
    even = parity == 0

    def sum2(e):
        total = fx * shift_x(e, 1) + fx_up * shift_x(e, -1)
        total = total + (fy * along(e, 1, 2) + fy_up * along(e, -1, 2))
        return total + (fz * along(e, 1, 1) + fz_up * along(e, -1, 1))

    e = jnp.where(even, source * inverse, 0.0)
    e = jnp.where(even, e, (source + sum2(e)) * inverse)
    resid = jnp.where(even, sum2(e), 0.0)

    def blocks(v, both_rows, both_layers):
        v = v.reshape(strips, x2, 8, 128)
        v = v[:, 0] + v[:, 1] if both_rows else v[:, 0]
        v = jnp.sum(v, axis=2, keepdims=True)
        v = jnp.broadcast_to(v, (strips, 8, 128))
        return v + along(v, -1, 1) if both_layers else v

    block[0, 0:strips] = blocks(resid, True, True)
    block[1, 0:strips] = blocks(store, True, True)
    block[2, 0:strips] = blocks(fx, False, True)
    block[2, strips] = jnp.zeros((8, 128), jnp.float32)
    block[3, 0:strips] = blocks(fz, True, False)
    solve_blocks(block, factors, answer, strips, slabs)
    add = jnp.broadcast_to(answer[...][:, None], (strips, x2, 8, 128)).reshape(shape)
    e = e + add
    e = jnp.where(even, (source + sum2(e)) * inverse, e)
    e = jnp.where(even, e, (source + sum2(e)) * inverse)
    e2[...] = jnp.zeros(e2.shape, jnp.float32)
    e2[x2 : x2 + rows2, 8:16, :] = e

    picked[...] = jnp.zeros(picked.shape, jnp.float32)
    for z in range(3 * z2):
        for x in range(3 * x2):
            at = z * 3 * x2 + x
            picked[at : at + 1, :] = e2[
                strip * x2 + x, pl.ds(8 - z2 + slab * z2 + z, 1), :
            ]
    spread_shape = (ny // 4, ny)
    spread = lax.broadcasted_iota(jnp.int32, spread_shape, 0) == (
        lax.broadcasted_iota(jnp.int32, spread_shape, 1) >> 2
    )
    wide[...] = jnp.dot(
        picked[...], jnp.where(spread, 1.0, 0.0), precision=HI, preferred_element_type=jnp.float32
    )

    zl1 = zl // 2
    small = (xl, ny)
    xo = (lax.broadcasted_iota(jnp.int32, small, 0) & 1) == 0
    yo = (lax.broadcasted_iota(jnp.int32, small, 1) & 1) == 0
    for zb in range(3):
        g = slab + (zb - 1)
        inside = jnp.logical_and(g >= 0, g < slabs)
        m = jnp.bitwise_xor(slab, jnp.clip(g, 0, slabs - 1))
        keep = jnp.where(inside, 1.0, 0.0)
        for which in range(3):
            xb = place(which, strip)
            tile = near[which][m]
            plane = jnp.concatenate(
                [tile[8 * c : 8 * c + 8, :] for c in range(ny // 128)], axis=1
            )
            plane = plane * keep
            for k in range(4):
                xk, yk = k // 2, k % 2
                v = jnp.where(jnp.logical_and(xo == (xk == 0), yo == (yk == 0)), plane, 0.0)
                v = v + roll(v, 1 if xk == 0 else -1, 0)
                v = v + roll(v, 1 if yk == 0 else -1, 1)
                e1[zb * zl1 + k, xb] = v
    window = (3 * xl, ny)
    for k in range(3 * zl1):
        rows = [wide[k // 2 * 3 * x2 + x : k // 2 * 3 * x2 + x + 1, :] for x in range(3 * x2)]
        rows = [jnp.broadcast_to(row, (4, ny)) for row in rows]
        rows = [jnp.concatenate(rows[x2 * b : x2 * b + x2], axis=0)[None] for b in range(3)]
        e1[k] = e1[k] + jnp.concatenate(rows, axis=0)

    def at1(k):
        return e1[k].reshape(window)

    xi = lax.broadcasted_iota(jnp.int32, window, 0)
    yi = lax.broadcasted_iota(jnp.int32, window, 1)
    parity0 = (xi + yi) & 1
    parity1 = ((xi >> 1) + (yi >> 1)) & 1

    def level1(k, colour):
        total = neighbour_sum(
            at1(k), at1(k - 1), at1(k + 1), fx1[k], fy1[k], fz1[k], fz1[k + 1], 2
        )
        updated = (src1[k] + total) * inv1[k]
        e1[k] = jnp.where(parity1 == ((k + colour) & 1), updated, at1(k)).reshape(3, xl, ny)

    def up1(colour, reach):
        def step(k, carry):
            level1(k, colour)
            return carry

        lax.fori_loop(zl1 - reach, 2 * zl1 + reach, step, 0, unroll=zl1 + 2 * reach)

    up1(0, 2)
    up1(1, 1)

    def join(i, carry):
        e0[i] = e0_in[i + zl - 2] + at1((zl - 2 + i) // 2)
        return carry

    lax.fori_loop(0, zl + 4, join, 0, unroll=6)

    def up0(colour, reach):
        def step(i, carry):
            z = i + zl - 2
            total = neighbour_sum(
                e0[i], e0[i - 1], e0[i + 1], fx0[z], fy0[z], fz0[z], fz0[z + 1], 1
            )
            updated = (src0[z] + total) * inv0[z]
            e0[i] = jnp.where(parity0 == ((i + colour) & 1), updated, e0[i])
            return carry

        lax.fori_loop(2 - reach, zl + 2 + reach, step, 0, unroll=zl + 2 * reach)

    up0(0, 1)
    up0(1, 0)
    for z in range(zl):
        out_ref[z] = head_ref[z] + e0[z + 2][xl : 2 * xl]


VMEM = pl.BlockSpec(memory_space=pltpu.VMEM)
SMEM = pl.BlockSpec(memory_space=pltpu.SMEM)


def f32(*shape):
    return jax.ShapeDtypeStruct(shape, jnp.float32)


def down(first, slabs, strips, zl, xl, ny, where, table, state, head=None, sat_old=None):
    zw, xw = 3 * zl, 3 * xl
    rows2 = 5 * (xl // 4) * (zl // 4)
    rows2 = -(-rows2 // 8) * 8
    out_shape = [f32(rows2 + 8 * ny // 128, 128)]
    out_shape += [f32(zw, xw, ny)] * 6 + [f32(zw // 2, xw, ny)] * 5
    operands = [where, table, *state]
    if first:
        out_shape.append(f32(zw, 3, xl, ny))
    else:
        operands += [*head, sat_old]
    split = pltpu.VMEM((zw, 3, xl, ny), jnp.float32)
    half = pltpu.VMEM((zw // 2, xw, ny), jnp.float32)
    return pl.pallas_call(
        functools.partial(down_kernel, first, slabs, strips, zl, xl),
        out_shape=out_shape,
        in_specs=[SMEM] + [VMEM] * (len(operands) - 1),
        out_specs=[VMEM] * len(out_shape),
        scratch_shapes=[split] * 4 + [half] * 2 + [pltpu.VMEM((rows2, ny), jnp.float32)],
        compiler_params=pltpu.CompilerParams(vmem_limit_bytes=30 * 1024 * 1024),
    )(*operands)


def up(slabs, strips, zl, xl, ny, where, pieces, near, kept, head):
    x2, z2 = xl // 4, zl // 4
    counts = [p.shape[0] for p in pieces]
    operands = [where, *pieces, *near, *kept, head]
    n = -(-9 * x2 * z2 // 8) * 8
    scratch = [
        pltpu.VMEM((5, strips * x2, 8, 128), jnp.float32),
        pltpu.VMEM((4, strips + 1, 8, 128), jnp.float32),
        pltpu.VMEM((strips, slabs * (slabs + 1), 1, 128), jnp.float32),
        pltpu.VMEM((strips, 8, 128), jnp.float32),
        pltpu.VMEM(((strips + 2) * x2, 24, 128), jnp.float32),
        pltpu.VMEM((n, ny // 4), jnp.float32),
        pltpu.VMEM((n, ny), jnp.float32),
        pltpu.VMEM((3 * zl // 2, 3, xl, ny), jnp.float32),
        pltpu.VMEM((zl + 4, 3 * xl, ny), jnp.float32),
    ]
    return pl.pallas_call(
        functools.partial(up_kernel, slabs, strips, zl, xl, counts),
        out_shape=f32(zl, xl, ny),
        in_specs=[SMEM] + [VMEM] * (len(operands) - 1),
        out_specs=VMEM,
        scratch_shapes=scratch,
        compiler_params=pltpu.CompilerParams(vmem_limit_bytes=30 * 1024 * 1024),
    )(*operands)


def swapped(x, axis, mask):
    return lax.ppermute(x, axis, [(i, i ^ mask) for i in range(lax.axis_size(axis))])


def crossed(x, strip_mask, slab_mask):
    strips, slabs = lax.axis_size("xy"), lax.axis_size("gz")
    pairs = [
        (i * slabs + j, (i ^ strip_mask) * slabs + (j ^ slab_mask))
        for i in range(strips)
        for j in range(slabs)
    ]
    return lax.ppermute(x, ("xy", "gz"), pairs)


def odd_pairs(x, axis):
    size = lax.axis_size(axis)
    pairs = [(i, i + 1) for i in range(1, size - 1, 2)]
    return lax.ppermute(x, axis, pairs + [(j, i) for i, j in pairs])


def neighbourhood(x):
    odd = odd_pairs(x, "xy")
    row = [x, swapped(x, "xy", 1), odd]
    far = [odd_pairs(v, "gz") for v in row]
    return row + [swapped(v, "gz", 1) for v in row] + far


def gather_strips(own, partner):
    size = lax.axis_size("xy")
    x = jnp.stack([own, partner])
    if size == 8:
        return [x] + [swapped(x, "xy", m) for m in (2, 4, 6)]
    mask = 2
    while mask < size:
        x = jnp.concatenate([x, swapped(x, "xy", mask)])
        mask *= 2
    return [x]


def per_device(head_old, soil_type, soil_table, land_mask, sun_bin):
    zl, xl, ny = head_old.shape
    strips, slabs = lax.axis_size("xy"), lax.axis_size("gz")
    where = jnp.stack([lax.axis_index("xy"), lax.axis_index("gz")]).astype(jnp.int32)
    resid, sat, alpha, shape_n, k_sat = soil_table
    table = jnp.stack([sat - resid, alpha, shape_n, k_sat, 1.0 - 1.0 / shape_n])
    table = jnp.pad(table, ((0, 3), (0, 128 - table.shape[1])))
    sun_share = jnp.maximum(0.0, jnp.sin(math.pi * (sun_bin.astype(jnp.float32) - 6.0) / 12.0))
    forcing = ET_PEAK * sun_share * land_mask.astype(jnp.float32)
    across = ((0, 0), (0, 0))
    soil = jnp.pad(soil_type, ((zl, 1), *across)).astype(jnp.float32)
    own = jnp.pad(head_old, ((0, zl + 1), *across)) + soil
    own = own + jnp.pad(forcing[None], ((2 * zl, 0), *across))
    state = neighbourhood(own)
    sizes = (slabs, strips, zl, xl, ny)
    base = -(-5 * (xl // 4) * (zl // 4) // 8) * 8

    def finish(payload, kept, head):
        pair = [payload, swapped(payload, "gz", 1)]
        pair = jnp.stack(pair)
        far = [crossed(pair, i, j) for i, j in ((0, 2), (1, 0), (1, 2))]
        full = jnp.concatenate([pair, far[0]])
        partner = jnp.concatenate([far[1], far[2]])
        pieces = gather_strips(full[:, :base], partner[:, :base])
        near = [full[:, base:], partner[:, base:], odd_pairs(full[:, base:], "xy")]
        return up(*sizes, where, pieces, near, kept, head)

    payload, *kept, sat_old = down(True, *sizes, where, table, state)
    head = finish(payload, kept, head_old)
    payload, *kept = down(
        False, *sizes, where, table, state, neighbourhood(head), sat_old
    )
    return finish(payload, kept, head)


def solution(mesh):
    in_specs = (P("gz", "xy", None), P("gz", "xy", None), P(), P("xy", None), P("xy", None))
    out_specs = P("gz", "xy", None)
    return jax.shard_map(
        per_device, mesh=mesh, in_specs=in_specs, out_specs=out_specs, check_vma=False
    )
```
